256 devices in a mesh: shard: 32 (over z, y_hi, core), replica: 8 (over y_lo, x).
Axes of the slice: x: 4, y: 4 (y_hi: 2, y_lo: 2; y = y_hi * 2 + y_lo), z: 8, core: 2. Of those that a mesh axis runs over, the one named last changes fastest.
Arguments:
- grad_vision: bfloat16 [8, 32, 256, 1280], P('replica', 'shard'), may hold values from -6 to 6
- grad_audio: bfloat16 [8, 32, 256, 1280], P('replica', 'shard'), may hold values from -6 to 6
- grad_lm: bfloat16 [8, 32, 256, 8192], P('replica', 'shard'), may hold values from -6 to 6
- master_vision: float32 [256, 1280], P('shard'), may hold values from -0.036 to 0.036
- master_audio: float32 [256, 1280], P('shard'), may hold values from -0.036 to 0.036
- master_lm: float32 [256, 8192], P('shard'), may hold values from -0.036 to 0.036
- moment_vision: float32 [256, 1280], P('shard'), may hold values from -0.018 to 0.018
- moment_audio: float32 [256, 1280], P('shard'), may hold values from -0.018 to 0.018
- moment_lm: float32 [256, 8192], P('shard'), may hold values from -0.018 to 0.018
- second_vision: float32 [256, 1280], P('shard'), may hold values from 1e-05 to 0.0001
- second_audio: float32 [256, 1280], P('shard'), may hold values from 1e-05 to 0.0001
- second_lm: float32 [256, 8192], P('shard'), may hold values from 1e-05 to 0.0001
- step_counts: int32 [3], replicated, may hold values from 1 to 8
Outputs:
- params_vision: bfloat16 [256, 1280], replicated
- params_audio: bfloat16 [256, 1280], replicated
- params_lm: bfloat16 [256, 8192], replicated
- new_master_vision: float32 [256, 1280], P('shard')
- new_master_audio: float32 [256, 1280], P('shard')
- new_master_lm: float32 [256, 8192], P('shard')
- new_moment_vision: float32 [256, 1280], P('shard')
- new_moment_audio: float32 [256, 1280], P('shard')
- new_moment_lm: float32 [256, 8192], P('shard')
- new_second_vision: float32 [256, 1280], P('shard')
- new_second_audio: float32 [256, 1280], P('shard')
- new_second_lm: float32 [256, 8192], P('shard')
The draws below stay inside these ranges and needn't reach their ends.
All inputs are finite; a program needn't handle non-finite values.
Results may differ from the reference program's by a relative error of at most 0.001.
Values may be sent and summed in bfloat16 or wider, within the bound.
A program may use at most 128 MiB of HBM per device.

```python
import math
import jax
import jax.numpy as jnp
from jax import lax

VW = 1280
AW = 1280
LW = 8192
VIS_ROWS = 256
AUD_ROWS = 256
LM_ROWS = 256
N_SHARD = 32
N_REPLICA = 8


def raised(result, key, source, target, shards_of, factor):
    owner, partner = [(jnp.arange(result.shape[axis_at]) // (result.shape[axis_at] // shards_of)).reshape([-1 if axis == axis_at else 1 for axis in range(result.ndim)]) for axis_at in (source, target)]
    chosen = jax.random.permutation(key, shards_of)[partner]
    strong = (owner == chosen) | (owner == (partner + shards_of // 2) % shards_of)
    return jnp.where(strong, factor * result, result)


def levels(stream_key, dims, shards, smallest, top_value):
    loudness, own = 1.0, jax.random.fold_in(stream_key, 6)
    for position, shards_of in shards:
        draws = jnp.exp(jax.random.uniform(jax.random.fold_in(own, position), (shards_of,), jnp.float32, smallest / len(shards), top_value / len(shards)))
        loudness = loudness * jnp.repeat(draws, dims[position] // shards_of).reshape([-1 if axis == position else 1 for axis in range(len(dims))])
    return loudness


def bell_draw(key, shape, scale, most, cuts=(), kind=jnp.bfloat16):
    values = jax.random.normal(key, shape, jnp.float32) * scale
    if len(cuts) > 0:
        values = levels(key, shape, cuts, -0.22, 0.18) * values
    return jnp.clip(values, min=-most, max=most).astype(kind)


def bell_draw_with(stream_key, shape, width, bound, shards, heavy, kind=jnp.bfloat16):
    array = width * jax.random.normal(stream_key, shape, jnp.float32)
    if shards:
        array = array * levels(stream_key, shape, shards, -0.22, 0.18)
    return jnp.clip(raised(array, jax.random.fold_in(stream_key, 3), *heavy), -bound, bound).astype(kind)


def setup_inputs(seed: int = 0) -> dict:
    key_of = jax.random.split(jax.random.key(seed), 14)
    return {
        "grad_vision": bell_draw_with(key_of[0], (N_REPLICA, N_SHARD, VIS_ROWS, VW), 1.0, 6.0, ((0, 8), (1, 32)), (1, 2, 32, 2.75)),
        "grad_audio": bell_draw_with(key_of[1], (N_REPLICA, N_SHARD, AUD_ROWS, AW), 1.0, 6.0, ((0, 8), (1, 32)), (1, 2, 32, 2.75)),
        "grad_lm": bell_draw_with(key_of[2], (N_REPLICA, N_SHARD, LM_ROWS, LW), 1.0, 6.0, ((0, 8), (1, 32)), (1, 2, 32, 2.75)),
        "master_vision": bell_draw(key_of[3], (VIS_ROWS, VW), 0.006, 0.036, ((0, 32),), jnp.float32),
        "master_audio": bell_draw(key_of[4], (AUD_ROWS, AW), 0.006, 0.036, ((0, 32),), jnp.float32),
        "master_lm": bell_draw(key_of[5], (LM_ROWS, LW), 0.006, 0.036, ((0, 32),), jnp.float32),
        "moment_vision": bell_draw(key_of[6], (VIS_ROWS, VW), 0.003, 0.018, ((0, 32),), jnp.float32),
        "moment_audio": bell_draw(key_of[7], (AUD_ROWS, AW), 0.003, 0.018, ((0, 32),), jnp.float32),
        "moment_lm": bell_draw(key_of[8], (LM_ROWS, LW), 0.003, 0.018, ((0, 32),), jnp.float32),
        "second_vision": jnp.clip(jnp.exp(math.log(0.0001) - 2.3025851 * jax.random.uniform(key_of[9], (VIS_ROWS, VW), jnp.float32) ** levels(key_of[9], (VIS_ROWS, VW), ((0, 32),), -0.2, 0.2)), 9.999999747378752e-06, 0.0001),
        "second_audio": jnp.clip(jnp.exp(math.log(0.0001) - 2.3025851 * jax.random.uniform(key_of[10], (AUD_ROWS, AW), jnp.float32) ** levels(key_of[10], (AUD_ROWS, AW), ((0, 32),), -0.2, 0.2)), 9.999999747378752e-06, 0.0001),
        "second_lm": jnp.clip(jnp.exp(math.log(0.0001) - 2.3025851 * jax.random.uniform(key_of[11], (LM_ROWS, LW), jnp.float32) ** levels(key_of[11], (LM_ROWS, LW), ((0, 32),), -0.2, 0.2)), 9.999999747378752e-06, 0.0001),
        "step_counts": jax.random.randint(key_of[12], (3,), 1, 9).astype(jnp.int32),
    }


BETA_ONE = 0.9
BETA_TWO = 0.95
EPSILON = 1e-08
WEIGHT_DECAY = 0.1
LEARN_RATE = 0.002

def bucket_sum(gradient):
    flat = gradient.reshape(-1, gradient.shape[2], gradient.shape[3])
    start = jnp.zeros((gradient.shape[2], gradient.shape[3]), jnp.float32)
    total, _ = lax.scan(lambda acc, piece: (acc + piece.astype(jnp.float32), None), start, flat)
    return total

def adamw_update(grad_sum, master, moment, second, count, devices_all):
    grad = grad_sum / devices_all
    moment_new = BETA_ONE * moment + (1.0 - BETA_ONE) * grad
    second_new = BETA_TWO * second + (1.0 - BETA_TWO) * grad * grad
    steps = count.astype(jnp.float32)
    first_fix = 1.0 - jnp.power(jnp.float32(BETA_ONE), steps)
    second_fix = 1.0 - jnp.power(jnp.float32(BETA_TWO), steps)
    update = moment_new / first_fix / (jnp.sqrt(second_new / second_fix) + EPSILON) + WEIGHT_DECAY * master
    master_new = master - LEARN_RATE * update
    return (master_new, moment_new, second_new)

def reference(grad_vision, grad_audio, grad_lm, master_vision, master_audio, master_lm, moment_vision, moment_audio, moment_lm, second_vision, second_audio, second_lm, step_counts):
    devices_all = float(N_SHARD * N_REPLICA)
    grads = (grad_vision, grad_audio, grad_lm)
    masters = (master_vision, master_audio, master_lm)
    moments = (moment_vision, moment_audio, moment_lm)
    seconds = (second_vision, second_audio, second_lm)
    results = [adamw_update(bucket_sum(grads[k]), masters[k], moments[k], seconds[k], step_counts[k], devices_all) for k in range(3)]
    return (results[0][0].astype(jnp.bfloat16), results[1][0].astype(jnp.bfloat16), results[2][0].astype(jnp.bfloat16), results[0][0], results[1][0], results[2][0], results[0][1], results[1][1], results[2][1], results[0][2], results[1][2], results[2][2])
```

```python
import math

import jax
import jax.numpy as jnp
from jax import lax
from jax.experimental import pallas as pl
from jax.experimental.pallas import tpu as pltpu
from jax.sharding import PartitionSpec as P

BETA_ONE = 0.9
BETA_TWO = 0.95
EPSILON = 1e-08
WEIGHT_DECAY = 0.1
LEARN_RATE = 0.002
MESH = pl.DeviceIdType.MESH
N_SEMS = 480


def adamw_update(grad_sum, master, moment, second, steps, devices_all):
    grad = grad_sum * (1.0 / devices_all)
    moment_new = BETA_ONE * moment + (1.0 - BETA_ONE) * grad
    second_new = BETA_TWO * second + (1.0 - BETA_TWO) * grad * grad
    t = jnp.full(grad_sum.shape, steps, jnp.float32)
    first_fix = 1.0 - jnp.exp(t * math.log(BETA_ONE))
    second_fix = 1.0 - jnp.exp(t * math.log(BETA_TWO))
    update = (
        moment_new / first_fix / (jnp.sqrt(second_new / second_fix) + EPSILON)
        + WEIGHT_DECAY * master
    )
    master_new = master - LEARN_RATE * update
    return master_new, moment_new, second_new


def coordinates():
    s, r = lax.axis_index("shard"), lax.axis_index("replica")
    z, yh, c = lax.div(s, 4), lax.rem(lax.div(s, 2), 2), lax.rem(s, 2)
    yl, x = lax.div(r, 4), lax.rem(r, 4)
    return x, yh, yl, z, c


def device(x, y, z, c):
    return (z * 4 + lax.div(y, 2) * 2 + c, lax.rem(y, 2) * 4 + x)


def cols(start, size):
    return pl.ds(pl.multiple_of(start, 128), size)


def step_kernel(
    gv, ga, gl, mv, ma, ml, nv, na, nl, sv, sa_, sl, steps,
    pv, pa, pm, tv, ta, tl,
    own_a, own_b, own_c, got_a, got_b, got_c, sum_a, sum_b, sum_c,
    rm_a, lm_a, b_r2, b_l2, b_from_l, b_from_r, c_r2, c_l2, c_from_l, c_from_r,
    a1, a2_got, a3_all,
    b1, b1_r2, b1_l2, b1_from_l, b1_from_r, b2, b3_got,
    c1, rm_c, lm_c, c2, c3_got,
    st_a, st_b, st_c, totals, all_a, all_b, all_c, sems,
):
    x, yh, yl, z, c = coordinates()
    y = yh * 2 + yl
    other = 1 - c
    f32 = jnp.float32

    def xj(j):
        return lax.rem(x + j, 4)

    def yj(j):
        return lax.rem(y + j, 4)

    def zj(j):
        return lax.rem(z + j, 8)

    core = device(x, y, z, other)
    right_x, left_x = device(xj(1), y, z, c), device(xj(3), y, z, c)
    right_y, left_y = device(x, yj(1), z, c), device(x, yj(3), z, c)
    right_z, left_z = device(x, y, zj(1), c), device(x, y, zj(7), c)
    y_twin = yh * 2 + (1 - yl)

    used = [0]
    started = []

    def sem():
        used[0] += 1
        return sems.at[used[0] - 1]

    def send(src, dst, to):
        copy = pltpu.make_async_remote_copy(
            src_ref=src, dst_ref=dst, send_sem=sem(), recv_sem=sem(),
            device_id=to, device_id_type=MESH,
        )
        copy.start()
        started.append(copy.wait_send)
        return copy

    def load(src, dst):
        copy = pltpu.make_async_copy(src, dst, sem())
        copy.start()
        return copy

    order = [("b", 2), ("c", 2), ("a", 4), ("b", 1), ("c", 1), ("a", 3), ("b", 3), ("c", 3), ("a", 5),
             ("a", 2), ("a", 6), ("a", 1), ("a", 7), ("b", 0), ("c", 0), ("a", 0)]

    def piece(part, j, half):
        if part == "b":
            yy = yj(j)
            at = gl.at[:, lax.div(yy, 2), :, cols(4096 * half + lax.rem(yy, 2) * 1024, 1024)]
            return [(at, lambda own, got: (own_b if own else got_b).at[j])]
        if part == "c":
            at = gl.at[:, :, :, cols(4096 * half + 2048 + xj(j) * 512, 512)]
            return [(at, lambda own, got: (own_c if own else got_c).at[j])]
        zz = zj(j)
        return [
            (gv.at[zz, :, :, cols(640 * half, 640)], lambda own, got: (own_a if own else got_a).at[j, :, :, pl.ds(0, 640)]),
            (ga.at[zz, :, :, cols(640 * half, 640)], lambda own, got: (own_a if own else got_a).at[j, :, :, pl.ds(640, 640)]),
        ]

    own_copies, core_copies = {}, {}
    for part, j in order:
        own_copies[part, j] = [load(src, dst(True, False)) for src, dst in piece(part, j, c)]

    col_a, col_b, col_c = yl * 640, yl * 1024 + x * 256, 2048 + x * 512 + yl * 256
    mine, theirs = pl.ds(pl.multiple_of(c * 8, 8), 8), pl.ds(pl.multiple_of(other * 8, 8), 8)

    def state_pieces(half):
        pairs = []
        for k, (v, a, m) in enumerate(((mv, ma, ml), (nv, na, nl), (sv, sa_, sl))):
            pairs.append((v.at[:, cols(640 * half, 640)], st_a.at[k, 0, mine]))
            pairs.append((a.at[:, cols(640 * half, 640)], st_a.at[k, 1, mine]))
            pairs.append((m.at[:, cols(4096 * half + col_b, 256)], st_b.at[k, mine]))
            pairs.append((m.at[:, cols(4096 * half + col_c, 256)], st_c.at[k, mine]))
        return pairs

    state_copies = [load(src, dst) for src, dst in state_pieces(c)]

    barrier = pltpu.get_barrier_semaphore()
    peers = [core]
    peers += [device(xj(k), y, z, c) for k in range(1, 4)]
    peers += [device(x, yj(k), z, c) for k in range(1, 4)]
    peers += [device(x, y, zj(k), c) for k in range(1, 8)]
    peers += [device(xj(k), y_twin, z, c) for k in range(1, 4)]
    for peer in peers:
        pl.semaphore_signal(barrier, inc=1, device_id=peer, device_id_type=MESH)
    pl.semaphore_wait(barrier, len(peers))

    for part, j in order:
        core_copies[part, j] = [send(src, dst(False, True), core) for src, dst in piece(part, j, other)]
    state_sends = [send(src, dst, core) for src, dst in state_pieces(other)]

    def chip_sum(part, j):
        for copy in own_copies[part, j]:
            copy.wait()
        for copy in core_copies[part, j]:
            copy.wait_recv()
        own, got, total = {"a": (own_a, got_a, sum_a), "b": (own_b, got_b, sum_b), "c": (own_c, got_c, sum_c)}[part]
        if part == "a":
            total[j] = own[j].astype(f32) + got[j].astype(f32)
        else:

            def body(i, _):
                total[j, i] = own[j, i].astype(f32) + got[j, i].astype(f32)
                return 0

            lax.fori_loop(0, 8, body, 0)

    lo, hi = pl.ds(0, 4), pl.ds(4, 4)

    def add_half(total, j, got, first):
        def body(i, _):
            total[j, first + i] = total[j, first + i] + got[i]
            return 0

        lax.fori_loop(0, 4, body, 0)

    class Ring4:
        def __init__(self, total, r2, l2, from_l, from_r, right, left):
            self.total, self.r2, self.l2, self.from_l, self.from_r = total, r2, l2, from_l, from_r
            self.right, self.left = right, left

        def far(self):
            self.c_r2 = send(self.total.at[2, lo], self.r2, self.right)
            self.c_l2 = send(self.total.at[2, hi], self.l2, self.left)

        def near_right(self):
            self.c_r_hi = send(self.total.at[1, hi], self.from_l.at[hi], self.right)

        def near_left(self):
            self.c_l_lo = send(self.total.at[3, lo], self.from_r.at[lo], self.left)

        def pass_on(self):
            self.c_r2.wait_recv()
            add_half(self.total, 1, self.r2, 0)
            self.c_r_lo = send(self.total.at[1, lo], self.from_l.at[lo], self.right)
            self.c_l2.wait_recv()
            add_half(self.total, 3, self.l2, 4)
            self.c_l_hi = send(self.total.at[3, hi], self.from_r.at[hi], self.left)

        def wait(self):
            for copy in (self.c_r_hi, self.c_l_lo, self.c_r_lo, self.c_l_hi):
                copy.wait_recv()

    class Ring8:
        def __init__(self, total, rm, lm, width):
            self.total, self.rm, self.lm = total, rm, lm
            self.h = (pl.ds(0, width), pl.ds(width, width))
            self.r, self.l = {}, {}

        def send_right(self, j, h):
            at = (slice(None), slice(None), self.h[h])
            self.r[j - 1, h] = send(self.total.at[(j,) + at], self.rm.at[(j - 1,) + at], right_z)

        def send_left(self, j, h):
            at = (slice(None), slice(None), self.h[h])
            self.l[j - 1, h] = send(self.total.at[((8 - j) % 8,) + at], self.lm.at[(j - 1,) + at], left_z)

        def step(self, m, h):
            self.r[m, h].wait_recv()
            at = (slice(None), slice(None), self.h[h])
            self.total[(m,) + at] = self.total[(m,) + at] + self.rm[(m,) + at]
            self.send_right(m, h)
            self.l[m, 1 - h].wait_recv()
            at = (slice(None), slice(None), self.h[1 - h])
            self.total[(8 - m,) + at] = self.total[(8 - m,) + at] + self.lm[(m,) + at]
            self.send_left(m, 1 - h)

        def wait(self):
            for h in (0, 1):
                self.r[0, h].wait_recv()
                self.l[0, h].wait_recv()

    ring_b = Ring4(sum_b, b_r2, b_l2, b_from_l, b_from_r, right_y, left_y)
    ring_c = Ring4(sum_c, c_r2, c_l2, c_from_l, c_from_r, right_x, left_x)
    ring_a = Ring8(sum_a, rm_a, lm_a, 640)

    chip_sum("b", 2)
    ring_b.far()
    chip_sum("c", 2)
    ring_c.far()
    chip_sum("a", 4)
    ring_a.send_right(4, 0)
    ring_a.send_left(4, 1)
    chip_sum("b", 1)
    ring_b.near_right()
    chip_sum("c", 1)
    ring_c.near_right()
    chip_sum("a", 3)
    ring_a.send_right(3, 1)
    chip_sum("b", 3)
    ring_b.near_left()
    chip_sum("c", 3)
    ring_c.near_left()
    chip_sum("a", 5)
    ring_a.send_left(3, 0)
    ring_a.step(3, 0)
    chip_sum("a", 2)
    chip_sum("a", 6)
    ring_a.step(2, 1)
    chip_sum("a", 1)
    chip_sum("a", 7)
    ring_b.pass_on()
    ring_c.pass_on()
    ring_a.step(2, 0)
    ring_a.step(1, 1)
    chip_sum("b", 0)
    chip_sum("c", 0)
    chip_sum("a", 0)
    ring_a.step(1, 0)

    ring_a.wait()
    a1[...] = sum_a[0] + rm_a[0] + lm_a[0]
    a2_copies = []
    for k in range(1, 4):
        yy = yj(k)
        src = a1.at[lax.div(yy, 2), :, cols(lax.rem(yy, 2) * 640, 640)]
        a2_copies.append(send(src, a2_got.at[k - 1], device(x, yy, z, c)))

    ring_b.wait()
    ring_b1 = Ring4(b1, b1_r2, b1_l2, b1_from_l, b1_from_r, right_x, left_x)

    def take_b(j):
        at = cols(xj(j) * 256, 256)

        def body(i, _):
            b1[j, i] = sum_b[0, i, :, at] + b_from_l[i, :, at] + b_from_r[i, :, at]
            return 0

        lax.fori_loop(0, 8, body, 0)

    take_b(2)
    ring_b1.far()
    take_b(1)
    ring_b1.near_right()
    take_b(3)
    ring_b1.near_left()

    ring_c.wait()
    ring_c1 = Ring8(c1, rm_c, lm_c, 256)

    def take_c(j):
        zz = zj(j)
        c1[j] = sum_c[0, zz] + c_from_l[zz] + c_from_r[zz]

    take_c(4)
    ring_c1.send_right(4, 0)
    ring_c1.send_left(4, 1)
    take_c(3)
    ring_c1.send_right(3, 1)
    take_c(5)
    ring_c1.send_left(3, 0)
    take_b(0)

    for copy in a2_copies:
        copy.wait_recv()
    a3_all[x] = a1[yh, :, cols(yl * 640, 640)] + a2_got[0] + a2_got[1] + a2_got[2]
    a3_copies = [send(a3_all.at[x], a3_all.at[x], device(xj(k), y, z, c)) for k in range(1, 4)]

    ring_c1.step(3, 0)
    take_c(2)
    take_c(6)
    ring_c1.step(2, 1)
    ring_b1.pass_on()
    take_c(1)
    take_c(7)
    ring_c1.step(2, 0)
    take_c(0)
    ring_c1.step(1, 1)

    ring_b1.wait()

    def take_b1(i, _):
        b2[i] = b1[0, i] + b1_from_l[i] + b1_from_r[i]
        return 0

    lax.fori_loop(0, 8, take_b1, 0)
    b3_copies = [send(b2.at[zj(k)], b3_got.at[k - 1], device(x, y, zj(k), c)) for k in range(1, 8)]
    ring_c1.step(1, 0)
    ring_c1.wait()
    c2[...] = c1[0] + rm_c[0] + lm_c[0]
    c3_copies = []
    for k in range(1, 4):
        yy = yj(k)
        src = c2.at[lax.div(yy, 2), :, cols(lax.rem(yy, 2) * 256, 256)]
        c3_copies.append(send(src, c3_got.at[k - 1], device(x, yy, z, c)))

    for copy in state_copies:
        copy.wait()
    for copy in state_sends:
        copy.wait_recv()
    t_vision, t_audio, t_lm = (steps[k].astype(f32) for k in range(3))

    for copy in a3_copies:
        copy.wait_recv()
    total_a = (a3_all[0] + a3_all[1]) + (a3_all[2] + a3_all[3])
    totals[:, cols(yl * 640, 640)] = total_a
    t_a = jnp.where(yl == 0, t_vision, t_audio)
    new_a = adamw_update(total_a, st_a[0, yl], st_a[1, yl], st_a[2, yl], t_a, 256.0)[0]
    all_a[z, yh, :, cols(yl * 640, 640)] = new_a.astype(jnp.bfloat16)
    at = all_a.at[z, yh, :, cols(yl * 640, 640)]
    ya_copies = [send(at, at, device(x, yj(k), z, c)) for k in range(1, 4)]

    for copy in b3_copies:
        copy.wait_recv()
    total_b = b2[z]
    for k in range(7):
        total_b = total_b + b3_got[k]
    totals[:, cols(1280 + col_b, 256)] = total_b
    new_b = adamw_update(total_b, st_b[0], st_b[1], st_b[2], t_lm, 256.0)[0]
    all_b[y, z, :, cols(x * 256, 256)] = new_b.astype(jnp.bfloat16)
    at = all_b.at[y, z, :, cols(x * 256, 256)]
    zb_copies = [send(at, at, device(x, y, zj(k), c)) for k in (4, 3, 5, 2, 6, 1, 7)]

    for copy in c3_copies:
        copy.wait_recv()
    total_c = c2[yh, :, cols(yl * 256, 256)] + c3_got[0] + c3_got[1] + c3_got[2]
    totals[:, cols(1280 + col_c, 256)] = total_c
    new_c = adamw_update(total_c, st_c[0], st_c[1], st_c[2], t_lm, 256.0)[0]
    all_c[x, z, yh, :, cols(yl * 256, 256)] = new_c.astype(jnp.bfloat16)
    at = all_c.at[x, z, yh, :, cols(yl * 256, 256)]
    yc_copies = [send(at, at, device(x, yj(k), z, c)) for k in range(1, 4)]

    at_a, at_b, at_c = (totals.at[:, cols(o, w)] for o, w in ((col_a, 640), (1280 + col_b, 256), (1280 + col_c, 256)))
    total_copies = [send(at_a, at_a, device(x, y_twin, z, c))]
    for k in range(4):
        for yy in (y, y_twin):
            if k or yy is not y:
                total_copies.append(send(at_b, at_b, device(xj(k), yy, z, c)))
                total_copies.append(send(at_c, at_c, device(xj(k), yy, z, c)))

    class Gather4:
        def __init__(self, at, right, left, me):
            self.at, self.me = at, me
            self.right, self.left = right, left

        def start(self):
            own = self.at(self.me, None)
            self.r = send(own, own, self.right)
            self.l = send(own, own, self.left)

        def pass_on(self):
            self.r.wait_recv()
            at = self.at(lax.rem(self.me + 3, 4), lo)
            self.r2 = send(at, at, self.right)
            self.l.wait_recv()
            at = self.at(lax.rem(self.me + 1, 4), hi)
            self.l2 = send(at, at, self.left)

        def wait(self):
            self.r2.wait_recv()
            self.l2.wait_recv()

    class Gather8:
        def __init__(self, at):
            self.at = at

        def start(self):
            own = self.at(z, None)
            self.r = send(own, own, right_z)
            self.l = send(own, own, left_z)

        def pass_on(self, k):
            self.r.wait_recv()
            at = self.at(zj(8 - k), 0 if k == 3 else None)
            self.r = send(at, at, right_z)
            self.l.wait_recv()
            at = self.at(zj(k), 1 if k == 3 else None)
            self.l = send(at, at, left_z)

        def wait(self):
            self.r.wait_recv()
            self.l.wait_recv()

    def at_a8(zz, h):
        if h is None:
            return all_a.at[zz]
        return all_a.at[zz, :, :, pl.ds(640 * h, 640)]

    def at_c8(zz, h):
        if h is None:
            return all_c.at[x, zz]
        return all_c.at[x, zz, :, :, pl.ds(256 * h, 256)]

    def at_bx(xx, h):
        return all_b.at[y, slice(None) if h is None else h, :, cols(xx * 256, 256)]

    def at_by(yy, h):
        return all_b.at[yy] if h is None else all_b.at[yy, h]

    def at_cx(xx, h):
        return all_c.at[xx] if h is None else all_c.at[xx, h]

    outs = []

    def put(src, dst):
        outs.append(load(src, dst))
        outs.append(send(src, dst, core))

    def put_b(yy):
        put(all_b.at[yy], pm.at[:, lax.div(yy, 2), :, cols(4096 * c + lax.rem(yy, 2) * 1024, 1024)])

    def put_c(xx):
        put(all_c.at[xx], pm.at[:, :, :, cols(4096 * c + 2048 + xx * 512, 512)])

    gather_a, gather_c = Gather8(at_a8), Gather8(at_c8)
    gather_b, gather_by = Gather4(at_bx, right_x, left_x, x), Gather4(at_by, right_y, left_y, y)
    gather_cx = Gather4(at_cx, right_x, left_x, x)

    for copy in ya_copies:
        copy.wait_recv()
    gather_a.start()
    for copy in yc_copies:
        copy.wait_recv()
    gather_c.start()
    for copy in zb_copies:
        copy.wait_recv()
    gather_b.start()
    gather_a.pass_on(1)
    gather_c.pass_on(1)
    gather_b.pass_on()
    gather_c.pass_on(2)
    gather_a.pass_on(2)
    gather_b.wait()
    gather_by.start()
    put_b(y)
    gather_c.pass_on(3)
    gather_a.pass_on(3)
    gather_c.wait()
    gather_cx.start()
    put_c(x)

    for copy in total_copies:
        copy.wait_recv()
    for first, width, out in ((0, 640, tv), (640, 640, ta), (1280, 4096, tl)):
        at = out.at[:, cols(width * c, width)]
        outs.append(load(totals.at[mine, pl.ds(first, width)], at))
        outs.append(send(totals.at[theirs, pl.ds(first, width)], at, core))

    gather_a.wait()
    put(all_a.at[:, :, :, pl.ds(0, 640)], pv.at[:, :, :, cols(640 * c, 640)])
    put(all_a.at[:, :, :, pl.ds(640, 640)], pa.at[:, :, :, cols(640 * c, 640)])
    gather_by.pass_on()
    put_b(yj(1))
    put_b(yj(3))
    gather_cx.pass_on()
    put_c(xj(1))
    put_c(xj(3))
    gather_by.wait()
    put_b(yj(2))
    gather_cx.wait()
    put_c(xj(2))

    for copy in outs:
        if copy.is_remote:
            copy.wait_recv()
        else:
            copy.wait()
    for wait_send in started:
        wait_send()


def whole_step(grads, states, step_counts):
    bf, f32 = jnp.bfloat16, jnp.float32
    vm = pltpu.VMEM
    scratch = [
        vm((8, 2, 16, 1280), bf), vm((4, 8, 16, 1024), bf), vm((4, 8, 2, 16, 512), bf),
        vm((8, 2, 16, 1280), bf), vm((4, 8, 16, 1024), bf), vm((4, 8, 2, 16, 512), bf),
        vm((8, 2, 16, 1280), f32), vm((4, 8, 16, 1024), f32), vm((4, 8, 2, 16, 512), f32),
        vm((4, 2, 16, 1280), f32), vm((4, 2, 16, 1280), f32),
        vm((4, 16, 1024), f32), vm((4, 16, 1024), f32), vm((8, 16, 1024), f32), vm((8, 16, 1024), f32),
        vm((4, 2, 16, 512), f32), vm((4, 2, 16, 512), f32), vm((8, 2, 16, 512), f32), vm((8, 2, 16, 512), f32),
        vm((2, 16, 1280), f32), vm((3, 16, 640), f32), vm((4, 16, 640), f32),
        vm((4, 8, 16, 256), f32), vm((4, 16, 256), f32), vm((4, 16, 256), f32),
        vm((8, 16, 256), f32), vm((8, 16, 256), f32), vm((8, 16, 256), f32), vm((7, 16, 256), f32),
        vm((8, 2, 16, 512), f32), vm((4, 2, 16, 512), f32), vm((4, 2, 16, 512), f32),
        vm((2, 16, 512), f32), vm((3, 16, 256), f32),
        vm((3, 2, 16, 640), f32), vm((3, 16, 256), f32), vm((3, 16, 256), f32), vm((16, 5376), f32),
        vm((8, 2, 16, 1280), bf), vm((4, 8, 16, 1024), bf), vm((4, 8, 2, 16, 512), bf),
        pltpu.SemaphoreType.DMA((N_SEMS,)),
    ]
    anywhere = pl.BlockSpec(memory_space=pl.ANY)
    return pl.pallas_call(
        step_kernel,
        out_shape=[
            jax.ShapeDtypeStruct((8, 2, 16, 1280), bf),
            jax.ShapeDtypeStruct((8, 2, 16, 1280), bf),
            jax.ShapeDtypeStruct((8, 2, 16, 8192), bf),
            jax.ShapeDtypeStruct((8, 1280), f32),
            jax.ShapeDtypeStruct((8, 1280), f32),
            jax.ShapeDtypeStruct((8, 8192), f32),
        ],
        in_specs=[anywhere] * 12 + [pl.BlockSpec(memory_space=pltpu.SMEM)],
        out_specs=[anywhere] * 6,
        scratch_shapes=scratch,
        compiler_params=pltpu.CompilerParams(
            collective_id=0, has_side_effects=True, vmem_limit_bytes=40 * 2**20
        ),
        name="sum_update_gather",
    )(*grads, *states, step_counts)


def state_kernel(tv, ta, tl, mv, ma, ml, nv, na, nl, sv, sa, sl, steps, *outs):
    for k, (t, m, n, s) in enumerate(((tv, mv, nv, sv), (ta, ma, na, sa), (tl, ml, nl, sl))):
        count = steps[k].astype(jnp.float32)
        new = adamw_update(t[...], m[...], n[...], s[...], count, 256.0)
        outs[k][...], outs[3 + k][...], outs[6 + k][...] = new


def update_states(totals, states, step_counts):
    whole = pl.BlockSpec(memory_space=pltpu.VMEM)
    return pl.pallas_call(
        state_kernel,
        out_shape=[jax.ShapeDtypeStruct(s.shape, s.dtype) for s in states],
        in_specs=[whole] * 12 + [pl.BlockSpec(memory_space=pltpu.SMEM)],
        out_specs=[whole] * 9,
        compiler_params=pltpu.CompilerParams(vmem_limit_bytes=16 * 2**20),
        name="update_states",
    )(*totals, *states, step_counts)


def per_device(*arguments):
    grads, states, step_counts = arguments[:3], arguments[3:12], arguments[12]
    grads = [g.reshape(8, 2, 16, g.shape[-1]) for g in grads]
    pv, pa, pm, *totals = whole_step(grads, states, step_counts)
    new_states = update_states(totals, states, step_counts)
    params = [p.reshape(256, p.shape[-1]) for p in (pv, pa, pm)]
    return (*params, *new_states)


def solution(mesh):
    grad, state = P("replica", "shard", None, None), P("shard", None)
    return jax.shard_map(
        per_device,
        mesh=mesh,
        in_specs=(grad,) * 3 + (state,) * 9 + (P(),),
        out_specs=(P(),) * 3 + (state,) * 9,
        check_vma=False,
    )
```

```python
import math

import jax
import jax.numpy as jnp
from jax import lax
from jax.experimental import pallas as pl
from jax.experimental.pallas import tpu as pltpu
from jax.sharding import PartitionSpec as P

BETA_ONE = 0.9
BETA_TWO = 0.95
EPSILON = 1e-08
WEIGHT_DECAY = 0.1
LEARN_RATE = 0.002
MESH = pl.DeviceIdType.MESH
N_SEMS = 640


def adamw_update(grad_sum, master, moment, second, steps, devices_all):
    grad = grad_sum * (1.0 / devices_all)
    moment_new = BETA_ONE * moment + (1.0 - BETA_ONE) * grad
    second_new = BETA_TWO * second + (1.0 - BETA_TWO) * grad * grad
    t = jnp.full(grad_sum.shape, steps, jnp.float32)
    first_fix = 1.0 - jnp.exp(t * math.log(BETA_ONE))
    second_fix = 1.0 - jnp.exp(t * math.log(BETA_TWO))
    update = (
        moment_new / first_fix / (jnp.sqrt(second_new / second_fix) + EPSILON)
        + WEIGHT_DECAY * master
    )
    master_new = master - LEARN_RATE * update
    return master_new, moment_new, second_new


def coordinates():
    s, r = lax.axis_index("shard"), lax.axis_index("replica")
    z, yh, c = lax.div(s, 4), lax.rem(lax.div(s, 2), 2), lax.rem(s, 2)
    yl, x = lax.div(r, 4), lax.rem(r, 4)
    return x, yh, yl, z, c


def device(x, y, z, c):
    return (z * 4 + lax.div(y, 2) * 2 + c, lax.rem(y, 2) * 4 + x)


def cols(start, size):
    return pl.ds(pl.multiple_of(start, 128), size)


def step_kernel(
    gv, ga, gl, mv, ma, ml, nv, na, nl, sv, sa, sl, steps,
    pv, pa, pm, mv_out, ma_out, ml_out, nv_out, na_out, nl_out, sv_out, sa_out, sl_out,
    own_v, own_a, own_m, got_v, got_a, got_b, got_c, sum_a, sum_b, sum_c, rm_a, lm_a,
    b_r2, b_l2, b_from_l, b_from_r, c_r2, c_l2, c_from_l, c_from_r,
    a1, a2_got, a3_all, rm_b, lm_b, rm_c, lm_c, b2, b3_got, c2, c3_got,
    st_a, st_b, st_c, state_v, state_a, state_m, totals, total_v, total_a, total_m,
    all_a, new_b, new_c, counts, sems,
):
    x, yh, yl, z, c = coordinates()
    y = yh * 2 + yl
    other = 1 - c
    f32, bf = jnp.float32, jnp.bfloat16

    def xj(j):
        return lax.rem(x + j, 4)

    def yj(j):
        return lax.rem(y + j, 4)

    def zj(j):
        return lax.rem(z + j, 8)

    core = device(x, y, z, other)
    right_x, left_x = device(xj(1), y, z, c), device(xj(3), y, z, c)
    right_y, left_y = device(x, yj(1), z, c), device(x, yj(3), z, c)
    right_z, left_z = device(x, y, zj(1), c), device(x, y, zj(7), c)
    y_twin = yh * 2 + (1 - yl)

    used = [0]
    started = []

    def sem():
        used[0] += 1
        return sems.at[used[0] - 1]

    def send(src, dst, to):
        copy = pltpu.make_async_remote_copy(
            src_ref=src, dst_ref=dst, send_sem=sem(), recv_sem=sem(),
            device_id=to, device_id_type=MESH,
        )
        copy.start()
        started.append(copy.wait_send)
        return copy

    def load(src, dst):
        copy = pltpu.make_async_copy(src, dst, sem())
        copy.start()
        return copy

    barrier = pltpu.get_barrier_semaphore()
    peers = [core]
    peers += [device(x, y, zj(k), c) for k in (2, 6, 1, 7)]
    peers += [device(xj(k), y, z, c) for k in range(1, 4)]
    peers += [device(x, yj(k), z, c) for k in range(1, 4)]
    peers += [device(xj(k), y_twin, z, c) for k in range(1, 4)]
    for peer in peers:
        pl.semaphore_signal(barrier, inc=1, device_id=peer, device_id_type=MESH)
    own_copies = {
        "m": load(gl.at[:, :, :, cols(4096 * c, 4096)], own_m),
        "v": load(gv.at[:, :, :, cols(640 * c, 640)], own_v),
        "a": load(ga.at[:, :, :, cols(640 * c, 640)], own_a),
    }
    pl.semaphore_wait(barrier, len(peers))

    order = [("b", 2), ("c", 2), ("b", 1), ("c", 1), ("b", 3), ("c", 3), ("v", 0), ("a", 0), ("b", 0), ("c", 0)]
    core_copies, taken = {}, set()

    def core_send():
        if len(core_copies) == len(order):
            return
        part, j = order[len(core_copies)]
        if part == "b":
            yy = yj(j)
            src = gl.at[:, lax.div(yy, 2), :, cols(4096 * other + lax.rem(yy, 2) * 1024, 1024)]
            dst = got_b.at[j]
        elif part == "c":
            src = gl.at[:, :, :, cols(4096 * other + 2048 + xj(j) * 512, 512)]
            dst = got_c.at[j]
        else:
            src = (gv if part == "v" else ga).at[:, :, :, cols(640 * other, 640)]
            dst = got_v if part == "v" else got_a
        core_copies[part, j] = send(src, dst, core)

    def take(own, part, j):
        if own not in taken:
            own_copies[own].wait()
            taken.add(own)
        if (part, j) not in taken:
            core_copies[part, j].wait_recv()
            core_send()
            taken.add((part, j))

    place = {4: 0, 3: 1, 5: 2, 2: 3, 6: 4, 1: 5, 7: 6, 0: 7}

    def z_at(p):
        return zj(4 + lax.div(p + 1, 2) * (2 * lax.rem(p + 1, 2) - 1))

    def chip_sum_b(j, first=0, n=8):
        take("m", "b", j)
        yy = yj(j)
        high, low = lax.div(yy, 2), lax.rem(yy, 2) * 1024

        def body(p, _):
            zz = z_at(p)
            for h in (0, 1):
                here = own_m[zz, high, :, cols(low + h * 512, 512)].astype(f32)
                sum_b[j, p, h] = here + got_b[j, zz, :, pl.ds(h * 512, 512)].astype(f32)
            return 0

        lax.fori_loop(first, first + n, body, 0)

    def chip_sum_c(j, first=0, n=8):
        take("m", "c", j)
        at = cols(2048 + xj(j) * 512, 512)

        def body(p, _):
            zz = z_at(p)
            for h in (0, 1):
                sum_c[j, p, h] = own_m[zz, h, :, at].astype(f32) + got_c[j, zz, h].astype(f32)
            return 0

        lax.fori_loop(first, first + n, body, 0)

    def chip_sum_a(j):
        zz = zj(j)
        sum_a[j, :, :, 0:640] = own_v[zz].astype(f32) + got_v[zz].astype(f32)
        sum_a[j, :, :, 640:1280] = own_a[zz].astype(f32) + got_a[zz].astype(f32)

    class Ring4:
        def __init__(self, piece, r2, l2, from_l, from_r, right, left):
            self.piece, self.r2, self.l2, self.from_l, self.from_r = piece, r2, l2, from_l, from_r
            self.right, self.left = right, left

        def far(self):
            self.c_r2 = send(self.piece(2, 0), self.r2, self.right)
            self.c_l2 = send(self.piece(2, 1), self.l2, self.left)

        def near_right(self):
            self.c_r1 = send(self.piece(1, 1), self.from_l(1), self.right)

        def near_left(self):
            self.c_l0 = send(self.piece(3, 0), self.from_r(0), self.left)

        def pass_on(self):
            self.c_r2.wait_recv()
            at = self.piece(1, 0)
            at[...] = at[...] + self.r2[...]
            self.c_r0 = send(at, self.from_l(0), self.right)
            self.c_l2.wait_recv()
            at = self.piece(3, 1)
            at[...] = at[...] + self.l2[...]
            self.c_l1 = send(at, self.from_r(1), self.left)

        def end(self):
            for copy in (self.c_r1, self.c_l0, self.c_r0, self.c_l1):
                copy.wait_recv()
            for h in (0, 1):
                at = self.piece(0, h)
                at[...] = at[...] + self.from_l(h)[...] + self.from_r(h)[...]

    class Ring8:
        def __init__(self, at, rm, lm):
            self.at, self.rm, self.lm = at, rm, lm
            self.r, self.l = {}, {}

        def send_right(self, m, h):
            self.r[m - 1, h] = send(self.at(m, h), self.rm(m - 1, h), right_z)

        def send_left(self, m, h):
            self.l[m - 1, h] = send(self.at((8 - m) % 8, h), self.lm(m - 1, h), left_z)

        def first(self):
            self.send_right(4, 0)
            self.send_left(4, 1)

        def second(self):
            self.send_right(3, 1)
            self.send_left(3, 0)

        def step(self, m, h):
            self.r[m, h].wait_recv()
            at = self.at(m, h)
            at[...] = at[...] + self.rm(m, h)[...]
            self.send_right(m, h)
            self.l[m, 1 - h].wait_recv()
            at = self.at(8 - m, 1 - h)
            at[...] = at[...] + self.lm(m, 1 - h)[...]
            self.send_left(m, 1 - h)

        def end(self, out):
            for h in (0, 1):
                self.r[0, h].wait_recv()
                self.l[0, h].wait_recv()
                out(h)[...] = self.at(0, h)[...] + self.rm(0, h)[...] + self.lm(0, h)[...]

    def ring4(total, r2, l2, from_l, from_r, right, left, first, n):
        at = pl.ds(first, n)
        return Ring4(
            lambda j, h: total.at[j, at, h], r2.at[at], l2.at[at],
            lambda h: from_l.at[at, h], lambda h: from_r.at[at, h], right, left,
        )

    def ring8(total, rm, lm):
        return Ring8(lambda m, h: total.at[0, place[m], h], lambda m, h: rm.at[m, h], lambda m, h: lm.at[m, h])

    def columns_a(ref):
        return lambda m, h: ref.at[m, :, :, pl.ds(640 * h, 640)]

    groups = ((0, 3), (3, 2), (5, 2), (7, 1))
    rb = [ring4(sum_b, b_r2, b_l2, b_from_l, b_from_r, right_y, left_y, *g) for g in groups]
    rc = [ring4(sum_c, c_r2, c_l2, c_from_l, c_from_r, right_x, left_x, *g) for g in groups]
    ring_a = Ring8(columns_a(sum_a), columns_a(rm_a), columns_a(lm_a))
    ring_b, ring_c = ring8(sum_b, rm_b, lm_b), ring8(sum_c, rm_c, lm_c)

    for _ in range(4):
        core_send()
    chip_sum_b(2, 0, 3)
    rb[0].far()
    chip_sum_c(2, 0, 3)
    rc[0].far()
    chip_sum_b(2, 3, 5)
    rb[1].far()
    chip_sum_c(2, 3, 5)
    rc[1].far()
    chip_sum_b(1)
    rb[0].near_right()
    chip_sum_c(1)
    rc[0].near_right()
    chip_sum_b(3)
    rb[0].near_left()
    chip_sum_c(3)
    rc[0].near_left()
    for ring in (rb[1], rc[1]):
        ring.near_right()
        ring.near_left()
    take("v", "v", 0)
    take("a", "a", 0)
    chip_sum_a(4)
    ring_a.first()
    rb[0].pass_on()
    rc[0].pass_on()
    chip_sum_a(3)
    chip_sum_a(5)
    ring_a.second()

    def first_sends(ring):
        ring.far()
        ring.near_right()
        ring.near_left()

    first_sends(rb[2])
    first_sends(rc[2])
    chip_sum_a(2)
    chip_sum_a(6)
    chip_sum_b(0)
    chip_sum_c(0)
    ring_a.step(3, 0)
    rb[1].pass_on()
    rc[1].pass_on()
    first_sends(rb[3])
    first_sends(rc[3])
    rb[0].end()
    ring_b.first()
    ring_b.second()
    rc[0].end()
    ring_c.first()
    ring_c.second()
    chip_sum_a(1)
    chip_sum_a(7)
    chip_sum_a(0)
    ring_a.step(2, 1)

    col_a, col_b, col_c = yl * 640, yl * 1024 + x * 256, 2048 + x * 512 + yl * 256
    mine, theirs = pl.ds(pl.multiple_of(c * 8, 8), 8), pl.ds(pl.multiple_of(other * 8, 8), 8)
    inputs = ((mv, ma, ml), (nv, na, nl), (sv, sa, sl))

    def state_pieces(half):
        pairs = []
        for k, (v, a, m) in enumerate(inputs):
            pairs.append((v.at[:, cols(640 * half, 640)], st_a.at[k, 0, mine]))
            pairs.append((a.at[:, cols(640 * half, 640)], st_a.at[k, 1, mine]))
            pairs.append((m.at[:, cols(4096 * half + col_b, 256)], st_b.at[k, mine]))
            pairs.append((m.at[:, cols(4096 * half + col_c, 256)], st_c.at[k, mine]))
        return pairs

    state_copies = [load(src, dst) for src, dst in state_pieces(c)] + [load(steps, counts)]
    state_sends = [send(src, dst, core) for src, dst in state_pieces(other)]
    for k, (v, a, m) in enumerate(inputs):
        state_copies += [load(v, state_v.at[k]), load(a, state_a.at[k]), load(m, state_m.at[k])]

    rb[2].pass_on()
    rc[2].pass_on()
    ring_a.step(2, 0)
    rb[1].end()
    ring_b.step(3, 0)
    ring_b.step(2, 1)
    rc[1].end()
    ring_c.step(3, 0)
    ring_c.step(2, 1)
    ring_a.step(1, 1)
    rb[3].pass_on()
    rc[3].pass_on()
    rb[2].end()
    rc[2].end()
    ring_b.step(1, 1)
    ring_c.step(1, 1)
    ring_b.step(2, 0)
    ring_c.step(2, 0)
    ring_a.step(1, 0)
    rb[3].end()
    rc[3].end()
    ring_b.step(1, 0)
    ring_c.step(1, 0)

    ring_a.end(lambda h: a1.at[:, :, pl.ds(640 * h, 640)])
    a2_copies = []
    for k in range(1, 4):
        yy = yj(k)
        src = a1.at[lax.div(yy, 2), :, cols(lax.rem(yy, 2) * 640, 640)]
        a2_copies.append(send(src, a2_got.at[k - 1], device(x, yy, z, c)))

    def owned(ref, i):
        return ref.at[lax.div(i, 2), :, cols(lax.rem(i, 2) * 256, 256)]

    ring_b.end(lambda h: b2.at[h])
    b3_copies = [send(owned(b2, xj(k)), b3_got.at[k - 1], device(xj(k), y, z, c)) for k in (2, 1, 3)]
    ring_c.end(lambda h: c2.at[h])
    c3_copies = [send(owned(c2, yj(k)), c3_got.at[k - 1], device(x, yj(k), z, c)) for k in (2, 1, 3)]
    for copy in a2_copies:
        copy.wait_recv()
    a3_all[x] = a1[yh, :, cols(yl * 640, 640)] + a2_got[0] + a2_got[1] + a2_got[2]
    a3_copies = [send(a3_all.at[x], a3_all.at[x], device(xj(k), y, z, c)) for k in range(1, 4)]

    for copy in state_copies:
        copy.wait()
    for copy in state_sends:
        copy.wait_recv()
    t_vision, t_audio, t_lm = (counts[k].astype(f32) for k in range(3))

    def at_b(yy, zz, h=None):
        first = 4096 * c + lax.rem(yy, 2) * 1024
        at = cols(first, 1024) if h is None else cols(first + 512 * h, 512)
        return pm.at[zz, lax.div(yy, 2), :, at]

    def at_c(xx, zz, h=None):
        return pm.at[zz, slice(None) if h is None else h, :, cols(4096 * c + 2048 + xx * 512, 512)]

    def update_owned(partial, i, got, copies, first, state, new):
        for copy in copies:
            copy.wait_recv()
        total = owned(partial, i)[...] + got[0] + got[1] + got[2]
        totals[:, cols(1280 + first, 256)] = total
        new[...] = adamw_update(total, state[0], state[1], state[2], t_lm, 256.0)[0].astype(bf)

    update_owned(b2, x, b3_got, b3_copies, col_b, st_b, new_b)
    at = pm.at[z, yh, :, cols(4096 * c + col_b, 256)]
    own_b = load(new_b, at)
    xb_copies = [send(new_b, at, device(xj(k), y, z, c)) for k in (2, 1, 3)]
    update_owned(c2, y, c3_got, c3_copies, col_c, st_c, new_c)
    at = pm.at[z, yh, :, cols(4096 * c + col_c, 256)]
    own_c = load(new_c, at)
    yc_copies = [send(new_c, at, device(x, yj(k), z, c)) for k in (2, 1, 3)]
    for copy in a3_copies:
        copy.wait_recv()
    total = (a3_all[0] + a3_all[1]) + (a3_all[2] + a3_all[3])
    totals[:, cols(yl * 640, 640)] = total
    t_a = jnp.where(yl == 0, t_vision, t_audio)
    updated = adamw_update(total, st_a[0, yl], st_a[1, yl], st_a[2, yl], t_a, 256.0)[0]
    all_a[z, yh, :, cols(yl * 640, 640)] = updated.astype(bf)
    at = all_a.at[z, yh, :, cols(yl * 640, 640)]
    ya_copies = [send(at, at, device(x, yj(k), z, c)) for k in (2, 1, 3)]

    class Relay4:
        def __init__(self, at, right, left, me, by_right):
            self.at, self.me, self.right, self.left, self.by_right = at, me, right, left, by_right

        def start(self):
            own = self.at(self.me)
            self.r = send(own, own, self.right)
            self.l = send(own, own, self.left)

        def pass_on(self):
            if self.by_right:
                self.r.wait_recv()
                at = self.at(lax.rem(self.me + 3, 4))
                self.far = send(at, at, self.right)
            else:
                self.l.wait_recv()
                at = self.at(lax.rem(self.me + 1, 4))
                self.far = send(at, at, self.left)

        def wait_near(self):
            (self.l if self.by_right else self.r).wait_recv()

    class Gather8:
        def __init__(self, at):
            self.at = at

        def start(self):
            own = self.at(z, None)
            self.r = send(own, own, right_z)
            self.l = send(own, own, left_z)

        def pass_on(self, k):
            self.r.wait_recv()
            at = self.at(zj(8 - k), 0 if k == 3 else None)
            self.r = send(at, at, right_z)
            self.l.wait_recv()
            at = self.at(zj(k), 1 if k == 3 else None)
            self.l = send(at, at, left_z)

        def wait(self):
            self.r.wait_recv()
            self.l.wait_recv()

    def at_a8(zz, h):
        if h is None:
            return all_a.at[zz]
        return all_a.at[zz, :, :, pl.ds(640 * h, 640)]

    class Block8:
        def __init__(self, at):
            self.at = at

        def start(self):
            own = self.at(z, None)
            self.r1, self.l1 = send(own, own, right_z), send(own, own, left_z)
            self.r2 = send(own, own, device(x, y, zj(2), c))
            self.l2 = send(own, own, device(x, y, zj(6), c))

        def near(self):
            self.r1.wait_recv()
            self.l1.wait_recv()

        def pass_on(self):
            self.r2.wait_recv()
            at, part = self.at(zj(6), None), self.at(zj(6), 0)
            self.r3 = send(at, at, right_z)
            self.r4 = send(part, part, device(x, y, zj(2), c))
            self.l2.wait_recv()
            at, part = self.at(zj(2), None), self.at(zj(2), 1)
            self.l3 = send(at, at, left_z)
            self.l4 = send(part, part, device(x, y, zj(6), c))

        def third(self):
            self.r3.wait_recv()
            self.l3.wait_recv()

        def fourth(self):
            self.r4.wait_recv()
            self.l4.wait_recv()

    outs = []

    def put(at):
        outs.append(send(at, at, core))

    def put_a(ref, first):
        src, dst = all_a.at[:, :, :, pl.ds(first, 640)], ref.at[:, :, :, cols(640 * c, 640)]
        outs.append(load(src, dst))
        outs.append(send(src, dst, core))

    def put_b(yy):
        put(pm.at[:, lax.div(yy, 2), :, cols(4096 * c + lax.rem(yy, 2) * 1024, 1024)])

    gather_a = Gather8(at_a8)
    gather_b, gather_c = Block8(lambda zz, h: at_b(y, zz, h)), Block8(lambda zz, h: at_c(x, zz, h))
    by = [Relay4(lambda i, m=m: at_b(i, zj(m)), right_y, left_y, y, m < 4) for m in range(8)]
    cx = [Relay4(lambda i, m=m: at_c(i, zj(m)), right_x, left_x, x, m < 4) for m in range(8)]

    def relays_start(*ms):
        for relays in (by, cx):
            for m in ms:
                relays[m].start()

    def relays_pass(*ms):
        for relays in (by, cx):
            for m in ms:
                relays[m].pass_on()

    own_b.wait()
    for copy in xb_copies:
        copy.wait_recv()
    by[0].start()
    gather_b.start()
    own_c.wait()
    for copy in yc_copies:
        copy.wait_recv()
    cx[0].start()
    gather_c.start()
    for copy in ya_copies:
        copy.wait_recv()
    gather_a.start()
    gather_b.near()
    gather_c.near()
    relays_start(1, 7)
    gather_b.pass_on()
    gather_c.pass_on()
    relays_start(2, 6)
    relays_pass(0)
    gather_a.pass_on(1)
    at_ta, at_tb, at_tc = (totals.at[:, cols(o, w)] for o, w in ((col_a, 640), (1280 + col_b, 256), (1280 + col_c, 256)))
    total_copies = [send(at_ta, at_ta, device(x, y_twin, z, c))]
    for k in range(4):
        for yy in (y, y_twin):
            if k or yy is not y:
                total_copies.append(send(at_tb, at_tb, device(xj(k), yy, z, c)))
                total_copies.append(send(at_tc, at_tc, device(xj(k), yy, z, c)))
    relays_pass(1, 7)
    gather_b.third()
    gather_c.third()
    relays_start(3, 5)
    gather_b.fourth()
    gather_c.fourth()
    relays_start(4)
    put_b(y)
    put(at_c(x, slice(None)))
    relays_pass(2, 6)
    gather_a.pass_on(2)
    relays_pass(3, 5)
    relays_pass(4)
    gather_a.pass_on(3)

    for copy in total_copies:
        copy.wait_recv()
    row_copies = []
    for first, width, out in ((0, 640, total_v), (640, 640, total_a), (1280, 4096, total_m)):
        at = out.at[:, cols(width * c, width)]
        row_copies.append(load(totals.at[mine, pl.ds(first, width)], at))
        row_copies.append(send(totals.at[theirs, pl.ds(first, width)], at, core))
    for relay in by + cx:
        relay.wait_near()
    put_b(yj(1))
    put_b(yj(3))
    put(at_c(xj(1), slice(None)))
    put(at_c(xj(3), slice(None)))
    for copy in row_copies:
        if copy.is_remote:
            copy.wait_recv()
        else:
            copy.wait()

    def update_state(total, state, t, at):
        new = adamw_update(total[:, at], state[0, :, at], state[1, :, at], state[2, :, at], t, 256.0)
        for k in range(3):
            state[k, :, at] = new[k]

    update_state(total_v, state_v, t_vision, pl.ds(0, 1280))
    update_state(total_a, state_a, t_audio, pl.ds(0, 1280))

    def update_columns(i, _):
        update_state(total_m, state_m, t_lm, cols(i * 1024, 1024))
        return 0

    lax.fori_loop(0, 8, update_columns, 0)
    new_states = ((mv_out, ma_out, ml_out), (nv_out, na_out, nl_out), (sv_out, sa_out, sl_out))
    for k, (v, a, m) in enumerate(new_states):
        outs += [load(state_v.at[k], v), load(state_a.at[k], a), load(state_m.at[k], m)]
    for m in (0, 1, 7, 2, 6, 3, 5, 4):
        by[m].far.wait_recv()
        put(at_b(yj(2), zj(m)))
        cx[m].far.wait_recv()
        put(at_c(xj(2), zj(m)))
    gather_a.wait()
    put_a(pv, 0)
    put_a(pa, 640)
    for copy in outs:
        if copy.is_remote:
            copy.wait_recv()
        else:
            copy.wait()
    for wait_send in started:
        wait_send()


def whole_step(grads, states, step_counts):
    bf, f32 = jnp.bfloat16, jnp.float32
    vm = pltpu.VMEM
    scratch = [
        vm((8, 2, 16, 640), bf), vm((8, 2, 16, 640), bf), vm((8, 2, 16, 4096), bf),
        vm((8, 2, 16, 640), bf), vm((8, 2, 16, 640), bf), vm((4, 8, 16, 1024), bf), vm((4, 8, 2, 16, 512), bf),
        vm((8, 2, 16, 1280), f32), vm((4, 8, 2, 16, 512), f32), vm((4, 8, 2, 16, 512), f32),
        vm((4, 2, 16, 1280), f32), vm((4, 2, 16, 1280), f32),
        *[vm((8, 16, 512), f32), vm((8, 16, 512), f32), vm((8, 2, 16, 512), f32), vm((8, 2, 16, 512), f32)] * 2,
        vm((2, 16, 1280), f32), vm((3, 16, 640), f32), vm((4, 16, 640), f32),
        *[vm((4, 2, 16, 512), f32)] * 4,
        *[vm((2, 16, 512), f32), vm((3, 16, 256), f32)] * 2,
        vm((3, 2, 16, 640), f32), vm((3, 16, 256), f32), vm((3, 16, 256), f32),
        vm((3, 8, 1280), f32), vm((3, 8, 1280), f32), vm((3, 8, 8192), f32),
        vm((16, 5376), f32), vm((8, 1280), f32), vm((8, 1280), f32), vm((8, 8192), f32),
        vm((8, 2, 16, 1280), bf), vm((16, 256), bf), vm((16, 256), bf),
        pltpu.SMEM((3,), jnp.int32),
        pltpu.SemaphoreType.DMA((N_SEMS,)),
    ]
    anywhere, hbm = pl.BlockSpec(memory_space=pl.ANY), pl.BlockSpec(memory_space=pltpu.HBM)
    shapes = [((8, 2, 16, g.shape[-1]), bf) for g in grads] + [(s.shape, f32) for s in states]
    return pl.pallas_call(
        step_kernel,
        out_shape=[pltpu.VMEM(*s) for s in shapes],
        in_specs=[hbm] * 13,
        out_specs=[anywhere] * 12,
        scratch_shapes=scratch,
        compiler_params=pltpu.CompilerParams(
            collective_id=0, has_side_effects=True, vmem_limit_bytes=32 * 2**20
        ),
        name="sum_update_gather",
    )(*[pltpu.with_memory_space_constraint(a, pltpu.HBM) for a in (*grads, *states, step_counts)])


def copy_kernel(*refs):
    n = len(refs) // 2
    sems = refs[-1]
    copies = [pltpu.make_async_copy(refs[k], refs[n + k], sems.at[k]) for k in range(n)]
    for copy in copies:
        copy.start()
    for copy in copies:
        copy.wait()


def copy_out(arrays):
    n = len(arrays)
    anywhere = pl.BlockSpec(memory_space=pl.ANY)
    return pl.pallas_call(
        copy_kernel,
        out_shape=[pltpu.HBM(a.shape, a.dtype) for a in arrays],
        in_specs=[anywhere] * n,
        out_specs=[anywhere] * n,
        scratch_shapes=[pltpu.SemaphoreType.DMA((n,))],
        compiler_params=pltpu.CompilerParams(vmem_limit_bytes=2**20),
        name="copy_out",
    )(*[pltpu.with_memory_space_constraint(a, pltpu.VMEM) for a in arrays])


def per_device(*arguments):
    grads, states, step_counts = arguments[:3], arguments[3:12], arguments[12]
    grads = [g.reshape(8, 2, 16, g.shape[-1]) for g in grads]
    results = copy_out(whole_step(grads, states, step_counts))
    return (*[p.reshape(256, p.shape[-1]) for p in results[:3]], *results[3:])


def solution(mesh):
    grad, state = P("replica", "shard", None, None), P("shard", None)
    return jax.shard_map(
        per_device,
        mesh=mesh,
        in_specs=(grad,) * 3 + (state,) * 9 + (P(),),
        out_specs=(P(),) * 3 + (state,) * 9,
        check_vma=False,
    )
```

```python
import math

import jax
import jax.numpy as jnp
from jax import lax
from jax.experimental import pallas as pl
from jax.experimental.pallas import tpu as pltpu
from jax.sharding import PartitionSpec as P

BETA_ONE = 0.9
BETA_TWO = 0.95
EPSILON = 1e-08
WEIGHT_DECAY = 0.1
LEARN_RATE = 0.002
MESH = pl.DeviceIdType.MESH
N_SEMS = 800


def adamw_update(grad_sum, master, moment, second, steps, devices_all):
    grad = grad_sum * (1.0 / devices_all)
    moment_new = BETA_ONE * moment + (1.0 - BETA_ONE) * grad
    second_new = BETA_TWO * second + (1.0 - BETA_TWO) * grad * grad
    t = jnp.full(grad_sum.shape, steps, jnp.float32)
    first_fix = 1.0 - jnp.exp(t * math.log(BETA_ONE))
    second_fix = 1.0 - jnp.exp(t * math.log(BETA_TWO))
    update = (
        moment_new / first_fix / (jnp.sqrt(second_new / second_fix) + EPSILON)
        + WEIGHT_DECAY * master
    )
    master_new = master - LEARN_RATE * update
    return master_new, moment_new, second_new


def coordinates():
    s, r = lax.axis_index("shard"), lax.axis_index("replica")
    z, yh, c = lax.div(s, 4), lax.rem(lax.div(s, 2), 2), lax.rem(s, 2)
    yl, x = lax.div(r, 4), lax.rem(r, 4)
    return x, yh, yl, z, c


def device(x, y, z, c):
    return (z * 4 + lax.div(y, 2) * 2 + c, lax.rem(y, 2) * 4 + x)


def cols(start, size):
    return pl.ds(pl.multiple_of(start, 128), size)


def step_kernel(
    gv, ga, gl, mv, ma, ml, nv, na, nl, sv, sa, sl, steps,
    pv, pa, pm, mv_out, ma_out, ml_out, nv_out, na_out, nl_out, sv_out, sa_out, sl_out,
    own_v, own_a, own_m, got_v, got_a, got_b, got_c, sum_a, sum_b, sum_c, rm_a, lm_a,
    b_r2, b_l2, b_from_l, b_from_r, c_r2, c_l2, c_from_l, c_from_r,
    a1, a2_got, a3_all, rm_b, lm_b, rm_c, lm_c, b2, b3_got, c2, c3_got,
    st_a, st_b, st_c, state_v, state_a, state_m, totals, total_v, total_a, total_m,
    all_a, new_b, new_c, counts, sems,
):
    x, yh, yl, z, c = coordinates()
    y = yh * 2 + yl
    other = 1 - c
    f32, bf = jnp.float32, jnp.bfloat16

    def xj(j):
        return lax.rem(x + j, 4)

    def yj(j):
        return lax.rem(y + j, 4)

    def zj(j):
        return lax.rem(z + j, 8)

    core = device(x, y, z, other)
    right_x, left_x = device(xj(1), y, z, c), device(xj(3), y, z, c)
    right_y, left_y = device(x, yj(1), z, c), device(x, yj(3), z, c)
    right_z, left_z = device(x, y, zj(1), c), device(x, y, zj(7), c)
    y_twin = yh * 2 + (1 - yl)

    used = [0]
    started = []

    def sem():
        used[0] += 1
        return sems.at[used[0] - 1]

    def send(src, dst, to):
        copy = pltpu.make_async_remote_copy(
            src_ref=src, dst_ref=dst, send_sem=sem(), recv_sem=sem(),
            device_id=to, device_id_type=MESH,
        )
        copy.start()
        started.append(copy.wait_send)
        return copy

    def seen():
        past = started[:]
        started.clear()
        return past

    def drain(past):
        for wait in past:
            wait()

    def load(src, dst):
        copy = pltpu.make_async_copy(src, dst, sem())
        copy.start()
        return copy

    barrier = pltpu.get_barrier_semaphore()
    peers = [core]
    peers += [device(x, y, zj(k), c) for k in (4, 3, 5, 2, 6, 1, 7)]
    peers += [device(xj(k), y, z, c) for k in range(1, 4)]
    peers += [device(x, yj(k), z, c) for k in range(1, 4)]
    peers += [device(xj(k), y_twin, z, c) for k in range(1, 4)]
    for peer in peers:
        pl.semaphore_signal(barrier, inc=1, device_id=peer, device_id_type=MESH)
    own_copies = {
        "m": load(gl.at[:, :, :, cols(4096 * c, 4096)], own_m),
        "v": load(gv.at[:, :, :, cols(640 * c, 640)], own_v),
        "a": load(ga.at[:, :, :, cols(640 * c, 640)], own_a),
    }
    pl.semaphore_wait(barrier, len(peers))

    order = [("a", 4), ("b", 2, 0, 3), ("c", 2, 0, 3), ("a", 3), ("a", 5), ("b", 2, 3, 5), ("c", 2, 3, 5), ("b", 1), ("c", 1),
             ("b", 3), ("c", 3), ("a", 2), ("a", 6), ("b", 0), ("c", 0), ("a", 1), ("a", 7), ("a", 0)]
    core_copies, taken = {}, set()

    place = {4: 0, 3: 1, 5: 2, 2: 3, 6: 4, 1: 5, 7: 6, 0: 7}

    def z_at(p):
        return zj(4 + lax.div(p + 1, 2) * (2 * lax.rem(p + 1, 2) - 1))

    def core_send():
        if len(core_copies) == len(order):
            return
        part, j, *blocks = piece = order[len(core_copies)]
        where = [z_at(jnp.int32(p)) for p in range(blocks[0], sum(blocks))] if blocks else [slice(None)]
        if part == "b":
            yy = yj(j)
            at = cols(4096 * other + lax.rem(yy, 2) * 1024, 1024)
            pairs = [(gl.at[zz, lax.div(yy, 2), :, at], got_b.at[j, zz]) for zz in where]
        elif part == "c":
            at = cols(4096 * other + 2048 + xj(j) * 512, 512)
            pairs = [(gl.at[zz, :, :, at], got_c.at[j, zz]) for zz in where]
        else:
            at = cols(640 * other, 640)
            pairs = [(gv.at[zj(j), :, :, at], got_v.at[j]), (ga.at[zj(j), :, :, at], got_a.at[j])]
        core_copies[piece] = [send(src, dst, core) for src, dst in pairs]

    def take(own, *piece):
        for name in own:
            if name not in taken:
                own_copies[name].wait()
                taken.add(name)
        for copy in core_copies[piece]:
            copy.wait_recv()
        core_send()

    def chip_sum_b(j, *blocks):
        take("m", "b", j, *blocks)
        first, n = blocks or (0, 8)
        yy = yj(j)
        high, low = lax.div(yy, 2), lax.rem(yy, 2) * 1024

        def body(p, _):
            zz = z_at(p)
            for h in (0, 1):
                here = own_m[zz, high, :, cols(low + h * 512, 512)].astype(f32)
                sum_b[j, p, h] = here + got_b[j, zz, :, pl.ds(h * 512, 512)].astype(f32)
            return 0

        lax.fori_loop(first, first + n, body, 0)

    def chip_sum_c(j, *blocks):
        take("m", "c", j, *blocks)
        first, n = blocks or (0, 8)
        at = cols(2048 + xj(j) * 512, 512)

        def body(p, _):
            zz = z_at(p)
            for h in (0, 1):
                sum_c[j, p, h] = own_m[zz, h, :, at].astype(f32) + got_c[j, zz, h].astype(f32)
            return 0

        lax.fori_loop(first, first + n, body, 0)

    def chip_sum_a(j):
        take("va", "a", j)
        zz = zj(j)
        sum_a[j, :, :, 0:640] = own_v[zz].astype(f32) + got_v[j].astype(f32)
        sum_a[j, :, :, 640:1280] = own_a[zz].astype(f32) + got_a[j].astype(f32)

    class Ring4:
        def __init__(self, piece, r2, l2, from_l, from_r, right, left):
            self.piece, self.r2, self.l2, self.from_l, self.from_r = piece, r2, l2, from_l, from_r
            self.right, self.left = right, left

        def far(self):
            self.c_r2 = send(self.piece(2, 0), self.r2, self.right)
            self.c_l2 = send(self.piece(2, 1), self.l2, self.left)

        def near_right(self):
            self.c_r1 = send(self.piece(1, 1), self.from_l(1), self.right)

        def near_left(self):
            self.c_l0 = send(self.piece(3, 0), self.from_r(0), self.left)

        def pass_on(self):
            self.c_r2.wait_recv()
            at = self.piece(1, 0)
            at[...] = at[...] + self.r2[...]
            self.c_r0 = send(at, self.from_l(0), self.right)
            self.c_l2.wait_recv()
            at = self.piece(3, 1)
            at[...] = at[...] + self.l2[...]
            self.c_l1 = send(at, self.from_r(1), self.left)

        def end(self):
            for copy in (self.c_r1, self.c_l0, self.c_r0, self.c_l1):
                copy.wait_recv()
            for h in (0, 1):
                at = self.piece(0, h)
                at[...] = at[...] + self.from_l(h)[...] + self.from_r(h)[...]

    class Ring8:
        def __init__(self, at, rm, lm):
            self.at, self.rm, self.lm = at, rm, lm
            self.r, self.l = {}, {}

        def send_right(self, m, h):
            self.r[m - 1, h] = send(self.at(m, h), self.rm(m - 1, h), right_z)

        def send_left(self, m, h):
            self.l[m - 1, h] = send(self.at((8 - m) % 8, h), self.lm(m - 1, h), left_z)

        def first(self):
            self.send_right(4, 0)
            self.send_left(4, 1)

        def second(self):
            self.send_right(3, 1)
            self.send_left(3, 0)

        def step(self, m, h):
            self.r[m, h].wait_recv()
            at = self.at(m, h)
            at[...] = at[...] + self.rm(m, h)[...]
            self.send_right(m, h)
            self.l[m, 1 - h].wait_recv()
            at = self.at(8 - m, 1 - h)
            at[...] = at[...] + self.lm(m, 1 - h)[...]
            self.send_left(m, 1 - h)

        def end(self, out):
            for h in (0, 1):
                self.r[0, h].wait_recv()
                self.l[0, h].wait_recv()
                out(h)[...] = self.at(0, h)[...] + self.rm(0, h)[...] + self.lm(0, h)[...]

    def ring4(total, r2, l2, from_l, from_r, right, left, first, n):
        at = pl.ds(first, n)
        return Ring4(
            lambda j, h: total.at[j, at, h], r2.at[at], l2.at[at],
            lambda h: from_l.at[at, h], lambda h: from_r.at[at, h], right, left,
        )

    def ring8(total, rm, lm):
        return Ring8(lambda m, h: total.at[0, place[m], h], lambda m, h: rm.at[m, h], lambda m, h: lm.at[m, h])

    def columns_a(ref):
        return lambda m, h: ref.at[m, :, :, pl.ds(640 * h, 640)]

    groups = ((0, 3), (3, 2), (5, 2), (7, 1))
    rb = [ring4(sum_b, b_r2, b_l2, b_from_l, b_from_r, right_y, left_y, *g) for g in groups]
    rc = [ring4(sum_c, c_r2, c_l2, c_from_l, c_from_r, right_x, left_x, *g) for g in groups]
    ring_a = Ring8(columns_a(sum_a), columns_a(rm_a), columns_a(lm_a))
    ring_b, ring_c = ring8(sum_b, rm_b, lm_b), ring8(sum_c, rm_c, lm_c)

    for _ in range(6):
        core_send()
    chip_sum_a(4)
    ring_a.first()
    chip_sum_b(2, 0, 3)
    rb[0].far()
    chip_sum_c(2, 0, 3)
    rc[0].far()
    chip_sum_a(3)
    chip_sum_a(5)
    ring_a.second()
    chip_sum_b(2, 3, 5)
    rb[1].far()
    chip_sum_c(2, 3, 5)
    rc[1].far()
    chip_sum_b(1)
    rb[0].near_right()
    chip_sum_c(1)
    rc[0].near_right()
    chip_sum_b(3)
    rb[0].near_left()
    chip_sum_c(3)
    rc[0].near_left()
    for ring in (rb[1], rc[1]):
        ring.near_right()
        ring.near_left()
    ring_a.step(3, 0)
    rb[0].pass_on()
    rc[0].pass_on()

    def first_sends(ring):
        ring.far()
        ring.near_right()
        ring.near_left()

    first_sends(rb[2])
    first_sends(rc[2])
    chip_sum_a(2)
    chip_sum_a(6)
    ring_a.step(2, 1)
    rb[1].pass_on()
    rc[1].pass_on()
    first_sends(rb[3])
    first_sends(rc[3])
    chip_sum_b(0)
    chip_sum_c(0)
    chip_sum_a(1)
    chip_sum_a(7)
    ring_a.step(2, 0)
    col_a, col_b, col_c = yl * 640, yl * 1024 + x * 256, 2048 + x * 512 + yl * 256
    mine, theirs = pl.ds(pl.multiple_of(c * 8, 8), 8), pl.ds(pl.multiple_of(other * 8, 8), 8)
    inputs = ((mv, ma, ml), (nv, na, nl), (sv, sa, sl))

    def state_pieces(half):
        pairs = []
        for k, (v, a, m) in enumerate(inputs):
            pairs.append((v.at[:, cols(640 * half, 640)], st_a.at[k, 0, mine]))
            pairs.append((a.at[:, cols(640 * half, 640)], st_a.at[k, 1, mine]))
            pairs.append((m.at[:, cols(4096 * half + col_b, 256)], st_b.at[k, mine]))
            pairs.append((m.at[:, cols(4096 * half + col_c, 256)], st_c.at[k, mine]))
        return pairs

    state_copies = [load(src, dst) for src, dst in state_pieces(c)] + [load(steps, counts)]
    state_sends = [send(src, dst, core) for src, dst in state_pieces(other)]
    for k, (v, a, m) in enumerate(inputs):
        state_copies += [load(v, state_v.at[k]), load(a, state_a.at[k]), load(m, state_m.at[k])]

    rb[0].end()
    ring_b.first()
    ring_b.second()
    rc[0].end()
    ring_c.first()
    ring_c.second()
    ring_a.step(1, 1)
    chip_sum_a(0)
    rb[2].pass_on()
    rc[2].pass_on()
    rb[3].pass_on()
    rc[3].pass_on()
    rb[1].end()
    rc[1].end()
    ring_b.step(3, 0)
    ring_c.step(3, 0)
    ring_a.step(1, 0)
    ring_b.step(2, 1)
    ring_c.step(2, 1)
    rb[2].end()
    rc[2].end()
    ring_b.step(2, 0)
    ring_c.step(2, 0)
    ring_b.step(1, 1)
    ring_c.step(1, 1)
    rb[3].end()
    rc[3].end()

    past = seen()
    ring_a.end(lambda h: a1.at[:, :, pl.ds(640 * h, 640)])
    a2_copies = []
    for k in range(1, 4):
        yy = yj(k)
        src = a1.at[lax.div(yy, 2), :, cols(lax.rem(yy, 2) * 640, 640)]
        a2_copies.append(send(src, a2_got.at[k - 1], device(x, yy, z, c)))
    ring_b.step(1, 0)
    ring_c.step(1, 0)

    def owned(ref, i):
        return ref.at[lax.div(i, 2), :, cols(lax.rem(i, 2) * 256, 256)]

    ring_b.end(lambda h: b2.at[h])
    b3_copies = [send(owned(b2, xj(k)), b3_got.at[k - 1], device(xj(k), y, z, c)) for k in (2, 1, 3)]
    ring_c.end(lambda h: c2.at[h])
    c3_copies = [send(owned(c2, yj(k)), c3_got.at[k - 1], device(x, yj(k), z, c)) for k in (2, 1, 3)]
    for copy in a2_copies:
        copy.wait_recv()
    a3_all[x] = a1[yh, :, cols(yl * 640, 640)] + a2_got[0] + a2_got[1] + a2_got[2]
    a3_copies = [send(a3_all.at[x], a3_all.at[x], device(xj(k), y, z, c)) for k in range(1, 4)]

    for copy in state_copies:
        copy.wait()
    for copy in state_sends:
        copy.wait_recv()
    t_vision, t_audio, t_lm = (counts[k].astype(f32) for k in range(3))

    def at_b(yy, zz, h=None):
        first = 4096 * c + lax.rem(yy, 2) * 1024
        at = cols(first, 1024) if h is None else cols(first + 512 * h, 512)
        return pm.at[zz, lax.div(yy, 2), :, at]

    def at_c(xx, zz, h=None):
        return pm.at[zz, slice(None) if h is None else h, :, cols(4096 * c + 2048 + xx * 512, 512)]

    def update_owned(partial, i, got, copies, first, state, new):
        for copy in copies:
            copy.wait_recv()
        total = owned(partial, i)[...] + got[0] + got[1] + got[2]
        totals[:, cols(1280 + first, 256)] = total
        new[...] = adamw_update(total, state[0], state[1], state[2], t_lm, 256.0)[0].astype(bf)

    update_owned(b2, x, b3_got, b3_copies, col_b, st_b, new_b)
    at = pm.at[z, yh, :, cols(4096 * c + col_b, 256)]
    own_b = load(new_b, at)
    b_z = {(8 - k) % 8: send(new_b, at, device(x, y, zj(k), c)) for k in (1, 7, 2, 6, 3, 5, 4)}
    b_last = {0: [send(new_b, at, device(xj(k), y, z, c)) for k in (2, 1, 3)]}
    update_owned(c2, y, c3_got, c3_copies, col_c, st_c, new_c)
    at = pm.at[z, yh, :, cols(4096 * c + col_c, 256)]
    own_c = load(new_c, at)
    c_z = {(8 - k) % 8: send(new_c, at, device(x, y, zj(k), c)) for k in (1, 7, 2, 6, 3, 5, 4)}
    c_last = {0: [send(new_c, at, device(x, yj(k), z, c)) for k in (2, 1, 3)]}
    for copy in a3_copies:
        copy.wait_recv()
    total = (a3_all[0] + a3_all[1]) + (a3_all[2] + a3_all[3])
    totals[:, cols(yl * 640, 640)] = total
    t_a = jnp.where(yl == 0, t_vision, t_audio)
    updated = adamw_update(total, st_a[0, yl], st_a[1, yl], st_a[2, yl], t_a, 256.0)[0]
    all_a[z, yh, :, cols(yl * 640, 640)] = updated.astype(bf)
    at = all_a.at[z, yh, :, cols(yl * 640, 640)]
    ya_copies = [send(at, at, device(x, yj(k), z, c)) for k in (2, 1, 3)]

    class Relay4:
        def __init__(self, at, right, left, me, by_right):
            self.at, self.me, self.right, self.left, self.by_right = at, me, right, left, by_right

        def start(self):
            own = self.at(self.me)
            self.r = send(own, own, self.right)
            self.l = send(own, own, self.left)

        def pass_on(self):
            if self.by_right:
                self.r.wait_recv()
                at = self.at(lax.rem(self.me + 3, 4))
                self.far = send(at, at, self.right)
            else:
                self.l.wait_recv()
                at = self.at(lax.rem(self.me + 1, 4))
                self.far = send(at, at, self.left)

        def wait_near(self):
            (self.l if self.by_right else self.r).wait_recv()

    class Gather8:
        def __init__(self, at):
            self.at = at

        def start(self):
            own = self.at(z, None)
            self.r = send(own, own, right_z)
            self.l = send(own, own, left_z)

        def pass_on(self, k):
            self.r.wait_recv()
            at = self.at(zj(8 - k), 0 if k == 3 else None)
            self.r = send(at, at, right_z)
            self.l.wait_recv()
            at = self.at(zj(k), 1 if k == 3 else None)
            self.l = send(at, at, left_z)

        def wait(self):
            self.r.wait_recv()
            self.l.wait_recv()

    def at_a8(zz, h):
        if h is None:
            return all_a.at[zz]
        return all_a.at[zz, :, :, pl.ds(640 * h, 640)]

    outs = []

    def put(at):
        outs.append(send(at, at, core))

    def put_a(zz):
        for ref, first in ((pv, 0), (pa, 640)):
            src, dst = all_a.at[zz, :, :, pl.ds(first, 640)], ref.at[zz, :, :, cols(640 * c, 640)]
            outs.append(load(src, dst))
            outs.append(send(src, dst, core))

    def put_b(yy):
        put(pm.at[:, lax.div(yy, 2), :, cols(4096 * c + lax.rem(yy, 2) * 1024, 1024)])

    gather_a = Gather8(at_a8)
    by = [Relay4(lambda i, m=m: at_b(i, zj(m)), right_y, left_y, y, m < 4) for m in range(8)]
    cx = [Relay4(lambda i, m=m: at_c(i, zj(m)), right_x, left_x, x, m < 4) for m in range(8)]

    def relays_pass(*ms):
        for relays in (by, cx):
            for m in ms:
                relays[m].pass_on()
        for relays, at, places in ((by, at_b, yj), (cx, at_c, xj)):
            for m in ms:
                relays[m].wait_near()
                put(at(places(1), zj(m)))
                put(at(places(3), zj(m)))

    def spread(*ms):
        for m in ms:
            b_z[m].wait_recv()
            at = pm.at[zj(m), yh, :, cols(4096 * c + col_b, 256)]
            b_last[m] = [send(at, at, device(xj(k), y, z, c)) for k in (2, 1, 3)]
            c_z[m].wait_recv()
            at = pm.at[zj(m), yh, :, cols(4096 * c + col_c, 256)]
            c_last[m] = [send(at, at, device(x, yj(k), z, c)) for k in (2, 1, 3)]

    def whole(*ms):
        for m in ms:
            for copy in b_last[m]:
                copy.wait_recv()
            by[m].start()
            for copy in c_last[m]:
                copy.wait_recv()
            cx[m].start()

    spread(1, 7)
    own_b.wait()
    own_c.wait()
    whole(0)
    spread(2, 6)
    for copy in ya_copies:
        copy.wait_recv()
    gather_a.start()
    put_a(z)
    drain(past)
    past = seen()
    spread(3, 5, 4)
    whole(1, 7)
    whole(2, 6)
    relays_pass(0)
    gather_a.pass_on(1)
    put_a(zj(7))
    put_a(zj(1))
    at_ta, at_tb, at_tc = (totals.at[:, cols(o, w)] for o, w in ((col_a, 640), (1280 + col_b, 256), (1280 + col_c, 256)))
    total_copies = [send(at_ta, at_ta, device(x, y_twin, z, c))]
    for k in range(4):
        for yy in (y, y_twin):
            if k or yy is not y:
                total_copies.append(send(at_tb, at_tb, device(xj(k), yy, z, c)))
                total_copies.append(send(at_tc, at_tc, device(xj(k), yy, z, c)))
    relays_pass(1, 7)
    drain(past)
    past = seen()
    whole(3, 5, 4)
    put_b(y)
    put(at_c(x, slice(None)))
    gather_a.pass_on(2)
    put_a(zj(6))
    put_a(zj(2))
    relays_pass(2, 6)
    relays_pass(3, 5)
    gather_a.pass_on(3)
    put_a(zj(5))
    put_a(zj(3))
    relays_pass(4)

    drain(past)
    past = seen()
    for copy in total_copies:
        copy.wait_recv()
    row_copies = []
    for first, width, out in ((0, 640, total_v), (640, 640, total_a), (1280, 4096, total_m)):
        at = out.at[:, cols(width * c, width)]
        row_copies.append(load(totals.at[mine, pl.ds(first, width)], at))
        row_copies.append(send(totals.at[theirs, pl.ds(first, width)], at, core))
    for copy in row_copies:
        if copy.is_remote:
            copy.wait_recv()
        else:
            copy.wait()

    def update_state(total, state, t, at):
        new = adamw_update(total[:, at], state[0, :, at], state[1, :, at], state[2, :, at], t, 256.0)
        for k in range(3):
            state[k, :, at] = new[k]

    update_state(total_v, state_v, t_vision, pl.ds(0, 1280))
    update_state(total_a, state_a, t_audio, pl.ds(0, 1280))

    def update_columns(i, _):
        update_state(total_m, state_m, t_lm, cols(i * 1024, 1024))
        return 0

    lax.fori_loop(0, 8, update_columns, 0)
    new_states = ((mv_out, ma_out, ml_out), (nv_out, na_out, nl_out), (sv_out, sa_out, sl_out))
    for k, (v, a, m) in enumerate(new_states):
        outs += [load(state_v.at[k], v), load(state_a.at[k], a), load(state_m.at[k], m)]
    drain(past)
    for m in (0, 1, 7, 2, 6, 3, 5, 4):
        by[m].far.wait_recv()
        put(at_b(yj(2), zj(m)))
        cx[m].far.wait_recv()
        put(at_c(xj(2), zj(m)))
    gather_a.wait()
    put_a(zj(4))
    for copy in outs:
        if copy.is_remote:
            copy.wait_recv()
        else:
            copy.wait()
    drain(seen())


def whole_step(grads, states, step_counts):
    bf, f32 = jnp.bfloat16, jnp.float32
    vm = pltpu.VMEM
    scratch = [
        vm((8, 2, 16, 640), bf), vm((8, 2, 16, 640), bf), vm((8, 2, 16, 4096), bf),
        vm((8, 2, 16, 640), bf), vm((8, 2, 16, 640), bf), vm((4, 8, 16, 1024), bf), vm((4, 8, 2, 16, 512), bf),
        vm((8, 2, 16, 1280), f32), vm((4, 8, 2, 16, 512), f32), vm((4, 8, 2, 16, 512), f32),
        vm((4, 2, 16, 1280), f32), vm((4, 2, 16, 1280), f32),
        *[vm((8, 16, 512), f32), vm((8, 16, 512), f32), vm((8, 2, 16, 512), f32), vm((8, 2, 16, 512), f32)] * 2,
        vm((2, 16, 1280), f32), vm((3, 16, 640), f32), vm((4, 16, 640), f32),
        *[vm((4, 2, 16, 512), f32)] * 4,
        *[vm((2, 16, 512), f32), vm((3, 16, 256), f32)] * 2,
        vm((3, 2, 16, 640), f32), vm((3, 16, 256), f32), vm((3, 16, 256), f32),
        vm((3, 8, 1280), f32), vm((3, 8, 1280), f32), vm((3, 8, 8192), f32),
        vm((16, 5376), f32), vm((8, 1280), f32), vm((8, 1280), f32), vm((8, 8192), f32),
        vm((8, 2, 16, 1280), bf), vm((16, 256), bf), vm((16, 256), bf),
        pltpu.SMEM((3,), jnp.int32),
        pltpu.SemaphoreType.DMA((N_SEMS,)),
    ]
    anywhere, hbm = pl.BlockSpec(memory_space=pl.ANY), pl.BlockSpec(memory_space=pltpu.HBM)
    shapes = [((8, 2, 16, g.shape[-1]), bf) for g in grads] + [(s.shape, f32) for s in states]
    return pl.pallas_call(
        step_kernel,
        out_shape=[pltpu.VMEM(*s) for s in shapes],
        in_specs=[hbm] * 13,
        out_specs=[anywhere] * 12,
        scratch_shapes=scratch,
        compiler_params=pltpu.CompilerParams(
            collective_id=0, has_side_effects=True, vmem_limit_bytes=32 * 2**20
        ),
        name="sum_update_gather",
    )(*[pltpu.with_memory_space_constraint(a, pltpu.HBM) for a in (*grads, *states, step_counts)])


def copy_kernel(*refs):
    n = len(refs) // 2
    sems = refs[-1]
    pairs = list(zip(refs[:n], refs[n:-1]))
    src, dst = pairs.pop(2)
    pairs = [(src.at[pl.ds(k, 2)], dst.at[pl.ds(k, 2)]) for k in (0, 2, 4, 6)] + pairs
    copies = [pltpu.make_async_copy(src, dst, sems.at[k]) for k, (src, dst) in enumerate(pairs)]
    for copy in copies:
        copy.start()
    for copy in copies:
        copy.wait()


def copy_out(arrays):
    n = len(arrays)
    anywhere = pl.BlockSpec(memory_space=pl.ANY)
    return pl.pallas_call(
        copy_kernel,
        out_shape=[pltpu.HBM(a.shape, a.dtype) for a in arrays],
        in_specs=[anywhere] * n,
        out_specs=[anywhere] * n,
        scratch_shapes=[pltpu.SemaphoreType.DMA((n + 3,))],
        compiler_params=pltpu.CompilerParams(vmem_limit_bytes=2**20),
        name="copy_out",
    )(*[pltpu.with_memory_space_constraint(a, pltpu.VMEM) for a in arrays])


def per_device(*arguments):
    grads, states, step_counts = arguments[:3], arguments[3:12], arguments[12]
    grads = [g.reshape(8, 2, 16, g.shape[-1]) for g in grads]
    results = copy_out(whole_step(grads, states, step_counts))
    return (*[p.reshape(256, p.shape[-1]) for p in results[:3]], *results[3:])


def solution(mesh):
    grad, state = P("replica", "shard", None, None), P("shard", None)
    return jax.shard_map(
        per_device,
        mesh=mesh,
        in_specs=(grad,) * 3 + (state,) * 9 + (P(),),
        out_specs=(P(),) * 3 + (state,) * 9,
        check_vma=False,
    )
```

```python
import math

import jax
import jax.numpy as jnp
from jax import lax
from jax.experimental import pallas as pl
from jax.experimental.pallas import tpu as pltpu
from jax.sharding import PartitionSpec as P

BETA_ONE = 0.9
BETA_TWO = 0.95
EPSILON = 1e-08
WEIGHT_DECAY = 0.1
LEARN_RATE = 0.002
MESH = pl.DeviceIdType.MESH
N_SEMS = 800


def adamw_update(grad_sum, master, moment, second, steps, devices_all):
    grad = grad_sum * (1.0 / devices_all)
    moment_new = BETA_ONE * moment + (1.0 - BETA_ONE) * grad
    second_new = BETA_TWO * second + (1.0 - BETA_TWO) * grad * grad
    t = jnp.full(grad_sum.shape, steps, jnp.float32)
    first_fix = 1.0 - jnp.exp(t * math.log(BETA_ONE))
    second_fix = 1.0 - jnp.exp(t * math.log(BETA_TWO))
    update = (
        moment_new / first_fix / (jnp.sqrt(second_new / second_fix) + EPSILON)
        + WEIGHT_DECAY * master
    )
    master_new = master - LEARN_RATE * update
    return master_new, moment_new, second_new


def coordinates():
    s, r = lax.axis_index("shard"), lax.axis_index("replica")
    z, yh, c = lax.div(s, 4), lax.rem(lax.div(s, 2), 2), lax.rem(s, 2)
    yl, x = lax.div(r, 4), lax.rem(r, 4)
    return x, yh, yl, z, c


def device(x, y, z, c):
    return (z * 4 + lax.div(y, 2) * 2 + c, lax.rem(y, 2) * 4 + x)


def cols(start, size):
    return pl.ds(pl.multiple_of(start, 128), size)


def step_kernel(
    gv, ga, gl, mv, ma, ml, nv, na, nl, sv, sa, sl, steps,
    pv, pa, pm, mv_out, ma_out, ml_out, nv_out, na_out, nl_out, sv_out, sa_out, sl_out,
    own_v, own_a, own_m, got_v, got_a, got_b, got_c, sum_a, sum_b, sum_c, rm_a, lm_a,
    b_r2, b_l2, b_from_l, b_from_r, c_r2, c_l2, c_from_l, c_from_r,
    a1, a2_got, a3_all, rm_b, lm_b, rm_c, lm_c, b2, b3_got, c2, c3_got,
    st_a, st_b, st_c, state_v, state_a, state_m, totals, total_v, total_a, total_m,
    all_a, new_b, new_c, counts, sems,
):
    x, yh, yl, z, c = coordinates()
    y = yh * 2 + yl
    other = 1 - c
    f32, bf = jnp.float32, jnp.bfloat16

    def xj(j):
        return lax.rem(x + j, 4)

    def yj(j):
        return lax.rem(y + j, 4)

    def zj(j):
        return lax.rem(z + j, 8)

    core = device(x, y, z, other)
    right_x, left_x = device(xj(1), y, z, c), device(xj(3), y, z, c)
    right_y, left_y = device(x, yj(1), z, c), device(x, yj(3), z, c)
    right_z, left_z = device(x, y, zj(1), c), device(x, y, zj(7), c)
    y_twin = yh * 2 + (1 - yl)

    used = [0]
    started = []

    def sem():
        used[0] += 1
        return sems.at[used[0] - 1]

    def send(src, dst, to):
        copy = pltpu.make_async_remote_copy(
            src_ref=src, dst_ref=dst, send_sem=sem(), recv_sem=sem(),
            device_id=to, device_id_type=MESH,
        )
        copy.start()
        started.append(copy.wait_send)
        return copy

    def seen():
        past = started[:]
        started.clear()
        return past

    def drain(past):
        for wait in past:
            wait()

    def load(src, dst):
        copy = pltpu.make_async_copy(src, dst, sem())
        copy.start()
        return copy

    barrier = pltpu.get_barrier_semaphore()
    peers = [core]
    peers += [device(x, y, zj(k), c) for k in (4, 3, 5, 2, 6, 1, 7)]
    peers += [device(xj(k), y, z, c) for k in range(1, 4)]
    peers += [device(x, yj(k), z, c) for k in range(1, 4)]
    peers += [device(xj(k), y_twin, z, c) for k in range(1, 4)]
    for peer in peers:
        pl.semaphore_signal(barrier, inc=1, device_id=peer, device_id_type=MESH)
    own_copies = {
        "m": load(gl.at[:, :, :, cols(4096 * c, 4096)], own_m),
        "v": load(gv.at[:, :, :, cols(640 * c, 640)], own_v),
        "a": load(ga.at[:, :, :, cols(640 * c, 640)], own_a),
    }
    pl.semaphore_wait(barrier, len(peers))

    order = [("a", 4), ("b", 2, 0, 3), ("c", 2, 0, 3), ("a", 3), ("a", 5), ("b", 2, 3, 5), ("c", 2, 3, 5), ("b", 1), ("c", 1),
             ("b", 3), ("c", 3), ("a", 2), ("a", 6), ("b", 0), ("c", 0), ("a", 1), ("a", 7), ("a", 0)]
    core_copies, taken = {}, set()

    place = {4: 0, 3: 1, 5: 2, 2: 3, 6: 4, 1: 5, 7: 6, 0: 7}

    def z_at(p):
        return zj(4 + lax.div(p + 1, 2) * (2 * lax.rem(p + 1, 2) - 1))

    def core_send():
        if len(core_copies) == len(order):
            return
        part, j, *blocks = piece = order[len(core_copies)]
        where = [z_at(jnp.int32(p)) for p in range(blocks[0], sum(blocks))] if blocks else [slice(None)]
        if part == "b":
            yy = yj(j)
            at = cols(4096 * other + lax.rem(yy, 2) * 1024, 1024)
            pairs = [(gl.at[zz, lax.div(yy, 2), :, at], got_b.at[j, zz]) for zz in where]
        elif part == "c":
            at = cols(4096 * other + 2048 + xj(j) * 512, 512)
            pairs = [(gl.at[zz, :, :, at], got_c.at[j, zz]) for zz in where]
        else:
            at = cols(640 * other, 640)
            pairs = [(gv.at[zj(j), :, :, at], got_v.at[j]), (ga.at[zj(j), :, :, at], got_a.at[j])]
        core_copies[piece] = [send(src, dst, core) for src, dst in pairs]

    def take(own, *piece):
        for name in own:
            if name not in taken:
                own_copies[name].wait()
                taken.add(name)
        for copy in core_copies[piece]:
            copy.wait_recv()
        core_send()

    def chip_sum_b(j, *blocks):
        take("m", "b", j, *blocks)
        first, n = blocks or (0, 8)
        yy = yj(j)
        high, low = lax.div(yy, 2), lax.rem(yy, 2) * 1024

        def body(p, _):
            zz = z_at(p)
            for h in (0, 1):
                here = own_m[zz, high, :, cols(low + h * 512, 512)].astype(f32)
                sum_b[j, p, h] = here + got_b[j, zz, :, pl.ds(h * 512, 512)].astype(f32)
            return 0

        lax.fori_loop(first, first + n, body, 0)

    def chip_sum_c(j, *blocks):
        take("m", "c", j, *blocks)
        first, n = blocks or (0, 8)
        at = cols(2048 + xj(j) * 512, 512)

        def body(p, _):
            zz = z_at(p)
            for h in (0, 1):
                sum_c[j, p, h] = own_m[zz, h, :, at].astype(f32) + got_c[j, zz, h].astype(f32)
            return 0

        lax.fori_loop(first, first + n, body, 0)

    def chip_sum_a(j):
        take("va", "a", j)
        zz = zj(j)
        sum_a[j, :, :, 0:640] = own_v[zz].astype(f32) + got_v[j].astype(f32)
        sum_a[j, :, :, 640:1280] = own_a[zz].astype(f32) + got_a[j].astype(f32)

    class Ring4:
        def __init__(self, piece, r2, l2, from_l, from_r, right, left):
            self.piece, self.r2, self.l2, self.from_l, self.from_r = piece, r2, l2, from_l, from_r
            self.right, self.left = right, left

        def far(self):
            self.c_r2 = send(self.piece(2, 0), self.r2, self.right)
            self.c_l2 = send(self.piece(2, 1), self.l2, self.left)

        def near_right(self):
            self.c_r1 = send(self.piece(1, 1), self.from_l(1), self.right)

        def near_left(self):
            self.c_l0 = send(self.piece(3, 0), self.from_r(0), self.left)

        def pass_on(self):
            self.c_r2.wait_recv()
            at = self.piece(1, 0)
            at[...] = at[...] + self.r2[...]
            self.c_r0 = send(at, self.from_l(0), self.right)
            self.c_l2.wait_recv()
            at = self.piece(3, 1)
            at[...] = at[...] + self.l2[...]
            self.c_l1 = send(at, self.from_r(1), self.left)

        def end(self):
            for copy in (self.c_r1, self.c_l0, self.c_r0, self.c_l1):
                copy.wait_recv()
            for h in (0, 1):
                at = self.piece(0, h)
                at[...] = at[...] + self.from_l(h)[...] + self.from_r(h)[...]

    class Ring8:
        def __init__(self, at, rm, lm):
            self.at, self.rm, self.lm = at, rm, lm
            self.r, self.l = {}, {}

        def send_right(self, m, h):
            self.r[m - 1, h] = send(self.at(m, h), self.rm(m - 1, h), right_z)

        def send_left(self, m, h):
            self.l[m - 1, h] = send(self.at((8 - m) % 8, h), self.lm(m - 1, h), left_z)

        def first(self):
            self.send_right(4, 0)
            self.send_left(4, 1)

        def second(self):
            self.send_right(3, 1)
            self.send_left(3, 0)

        def step(self, m, h):
            self.r[m, h].wait_recv()
            at = self.at(m, h)
            at[...] = at[...] + self.rm(m, h)[...]
            self.send_right(m, h)
            self.l[m, 1 - h].wait_recv()
            at = self.at(8 - m, 1 - h)
            at[...] = at[...] + self.lm(m, 1 - h)[...]
            self.send_left(m, 1 - h)

        def end(self, out):
            for h in (0, 1):
                self.r[0, h].wait_recv()
                self.l[0, h].wait_recv()
                out(h)[...] = self.at(0, h)[...] + self.rm(0, h)[...] + self.lm(0, h)[...]

    def ring4(total, r2, l2, from_l, from_r, right, left, first, n):
        at = pl.ds(first, n)
        return Ring4(
            lambda j, h: total.at[j, at, h], r2.at[at], l2.at[at],
            lambda h: from_l.at[at, h], lambda h: from_r.at[at, h], right, left,
        )

    def ring8(total, rm, lm):
        return Ring8(lambda m, h: total.at[0, place[m], h], lambda m, h: rm.at[m, h], lambda m, h: lm.at[m, h])

    def columns_a(ref):
        return lambda m, h: ref.at[m, :, :, pl.ds(640 * h, 640)]

    groups = ((0, 3), (3, 2), (5, 2), (7, 1))
    rb = [ring4(sum_b, b_r2, b_l2, b_from_l, b_from_r, right_y, left_y, *g) for g in groups]
    rc = [ring4(sum_c, c_r2, c_l2, c_from_l, c_from_r, right_x, left_x, *g) for g in groups]
    ring_a = Ring8(columns_a(sum_a), columns_a(rm_a), columns_a(lm_a))
    ring_b, ring_c = ring8(sum_b, rm_b, lm_b), ring8(sum_c, rm_c, lm_c)

    for _ in range(6):
        core_send()
    chip_sum_a(4)
    ring_a.first()
    chip_sum_b(2, 0, 3)
    rb[0].far()
    chip_sum_c(2, 0, 3)
    rc[0].far()
    chip_sum_a(3)
    chip_sum_a(5)
    ring_a.second()
    chip_sum_b(2, 3, 5)
    rb[1].far()
    chip_sum_c(2, 3, 5)
    rc[1].far()
    chip_sum_b(1)
    rb[0].near_right()
    chip_sum_c(1)
    rc[0].near_right()
    chip_sum_b(3)
    rb[0].near_left()
    chip_sum_c(3)
    rc[0].near_left()
    for ring in (rb[1], rc[1]):
        ring.near_right()
        ring.near_left()
    ring_a.step(3, 0)
    rb[0].pass_on()
    rc[0].pass_on()

    def first_sends(ring):
        ring.far()
        ring.near_right()
        ring.near_left()

    first_sends(rb[2])
    first_sends(rc[2])
    chip_sum_a(2)
    chip_sum_a(6)
    ring_a.step(2, 1)
    rb[1].pass_on()
    rc[1].pass_on()
    first_sends(rb[3])
    first_sends(rc[3])
    chip_sum_b(0)
    chip_sum_c(0)
    chip_sum_a(1)
    chip_sum_a(7)
    ring_a.step(2, 0)
    col_a, col_b, col_c = yl * 640, yl * 1024 + x * 256, 2048 + x * 512 + yl * 256
    mine, theirs = pl.ds(pl.multiple_of(c * 8, 8), 8), pl.ds(pl.multiple_of(other * 8, 8), 8)
    inputs = ((mv, ma, ml), (nv, na, nl), (sv, sa, sl))

    def state_pieces(half):
        pairs = []
        for k, (v, a, m) in enumerate(inputs):
            pairs.append((v.at[:, cols(640 * half, 640)], st_a.at[k, 0, mine]))
            pairs.append((a.at[:, cols(640 * half, 640)], st_a.at[k, 1, mine]))
            pairs.append((m.at[:, cols(4096 * half + col_b, 256)], st_b.at[k, mine]))
            pairs.append((m.at[:, cols(4096 * half + col_c, 256)], st_c.at[k, mine]))
        return pairs

    state_copies = [load(src, dst) for src, dst in state_pieces(c)] + [load(steps, counts)]
    state_sends = [send(src, dst, core) for src, dst in state_pieces(other)]
    for k, (v, a, m) in enumerate(inputs):
        state_copies += [load(v, state_v.at[k]), load(a, state_a.at[k]), load(m, state_m.at[k])]

    rb[0].end()
    ring_b.first()
    ring_b.second()
    rc[0].end()
    ring_c.first()
    ring_c.second()
    ring_a.step(1, 1)
    chip_sum_a(0)
    rb[2].pass_on()
    rc[2].pass_on()
    rb[3].pass_on()
    rc[3].pass_on()
    rb[1].end()
    rc[1].end()
    ring_b.step(3, 0)
    ring_c.step(3, 0)
    ring_a.step(1, 0)
    ring_b.step(2, 1)
    ring_c.step(2, 1)
    rb[2].end()
    rc[2].end()
    ring_b.step(2, 0)
    ring_c.step(2, 0)
    ring_b.step(1, 1)
    ring_c.step(1, 1)
    rb[3].end()
    rc[3].end()

    past = seen()
    ring_a.end(lambda h: a1.at[:, :, pl.ds(640 * h, 640)])
    a2_copies = []
    for k in range(1, 4):
        yy = yj(k)
        src = a1.at[lax.div(yy, 2), :, cols(lax.rem(yy, 2) * 640, 640)]
        a2_copies.append(send(src, a2_got.at[k - 1], device(x, yy, z, c)))
    ring_b.step(1, 0)
    ring_c.step(1, 0)

    def owned(ref, i):
        return ref.at[lax.div(i, 2), :, cols(lax.rem(i, 2) * 256, 256)]

    ring_b.end(lambda h: b2.at[h])
    b3_copies = [send(owned(b2, xj(k)), b3_got.at[k - 1], device(xj(k), y, z, c)) for k in (2, 1, 3)]
    ring_c.end(lambda h: c2.at[h])
    c3_copies = [send(owned(c2, yj(k)), c3_got.at[k - 1], device(x, yj(k), z, c)) for k in (2, 1, 3)]
    for copy in a2_copies:
        copy.wait_recv()
    a3_all[x] = a1[yh, :, cols(yl * 640, 640)] + a2_got[0] + a2_got[1] + a2_got[2]
    a3_copies = [send(a3_all.at[x], a3_all.at[x], device(xj(k), y, z, c)) for k in range(1, 4)]

    for copy in state_copies:
        copy.wait()
    for copy in state_sends:
        copy.wait_recv()
    t_vision, t_audio, t_lm = (counts[k].astype(f32) for k in range(3))

    def at_b(yy, zz, h=None):
        first = 4096 * c + lax.rem(yy, 2) * 1024
        at = cols(first, 1024) if h is None else cols(first + 512 * h, 512)
        return pm.at[zz, lax.div(yy, 2), :, at]

    def at_c(xx, zz, h=None):
        return pm.at[zz, slice(None) if h is None else h, :, cols(4096 * c + 2048 + xx * 512, 512)]

    def update_owned(partial, i, got, copies, first, state, new):
        for copy in copies:
            copy.wait_recv()
        total = owned(partial, i)[...] + got[0] + got[1] + got[2]
        totals[:, cols(1280 + first, 256)] = total
        new[...] = adamw_update(total, state[0], state[1], state[2], t_lm, 256.0)[0].astype(bf)

    update_owned(b2, x, b3_got, b3_copies, col_b, st_b, new_b)
    at = pm.at[z, yh, :, cols(4096 * c + col_b, 256)]
    own_b = load(new_b, at)
    b_z = {(8 - k) % 8: send(new_b, at, device(x, y, zj(k), c)) for k in (1, 7, 2, 6, 3, 5, 4)}
    b_last = {0: [send(new_b, at, device(xj(k), y, z, c)) for k in (2, 1, 3)]}
    update_owned(c2, y, c3_got, c3_copies, col_c, st_c, new_c)
    at = pm.at[z, yh, :, cols(4096 * c + col_c, 256)]
    own_c = load(new_c, at)
    c_z = {(8 - k) % 8: send(new_c, at, device(x, y, zj(k), c)) for k in (1, 7, 2, 6, 3, 5, 4)}
    c_last = {0: [send(new_c, at, device(x, yj(k), z, c)) for k in (2, 1, 3)]}
    for copy in a3_copies:
        copy.wait_recv()
    total = (a3_all[0] + a3_all[1]) + (a3_all[2] + a3_all[3])
    totals[:, cols(yl * 640, 640)] = total
    t_a = jnp.where(yl == 0, t_vision, t_audio)
    updated = adamw_update(total, st_a[0, yl], st_a[1, yl], st_a[2, yl], t_a, 256.0)[0]
    all_a[z, yh, :, cols(yl * 640, 640)] = updated.astype(bf)
    at = all_a.at[z, yh, :, cols(yl * 640, 640)]
    ya_copies = [send(at, at, device(x, yj(k), z, c)) for k in (2, 1, 3)]

    class Relay4:
        def __init__(self, at, right, left, me, by_right):
            self.at, self.me, self.right, self.left, self.by_right = at, me, right, left, by_right

        def start(self):
            own = self.at(self.me)
            self.r = send(own, own, self.right)
            self.l = send(own, own, self.left)

        def pass_on(self):
            if self.by_right:
                self.r.wait_recv()
                at = self.at(lax.rem(self.me + 3, 4))
                self.far = send(at, at, self.right)
            else:
                self.l.wait_recv()
                at = self.at(lax.rem(self.me + 1, 4))
                self.far = send(at, at, self.left)

        def wait_near(self):
            (self.l if self.by_right else self.r).wait_recv()

    class Gather8:
        def __init__(self, at):
            self.at = at

        def start(self):
            own = self.at(z, None)
            self.r = send(own, own, right_z)
            self.l = send(own, own, left_z)

        def pass_on(self, k):
            self.r.wait_recv()
            at = self.at(zj(8 - k), 0 if k == 3 else None)
            self.r = send(at, at, right_z)
            self.l.wait_recv()
            at = self.at(zj(k), 1 if k == 3 else None)
            self.l = send(at, at, left_z)

        def wait(self):
            self.r.wait_recv()
            self.l.wait_recv()

    def at_a8(zz, h):
        if h is None:
            return all_a.at[zz]
        return all_a.at[zz, :, :, pl.ds(640 * h, 640)]

    outs = []

    def put(at):
        outs.append(send(at, at, core))

    def put_a(zz):
        for ref, first in ((pv, 0), (pa, 640)):
            src, dst = all_a.at[zz, :, :, pl.ds(first, 640)], ref.at[zz, :, :, cols(640 * c, 640)]
            outs.append(load(src, dst))
            outs.append(send(src, dst, core))

    def put_b(yy):
        put(pm.at[:, lax.div(yy, 2), :, cols(4096 * c + lax.rem(yy, 2) * 1024, 1024)])

    gather_a = Gather8(at_a8)
    by = [Relay4(lambda i, m=m: at_b(i, zj(m)), right_y, left_y, y, m < 4) for m in range(8)]
    cx = [Relay4(lambda i, m=m: at_c(i, zj(m)), right_x, left_x, x, m < 4) for m in range(8)]

    def relays_pass(*ms):
        for relays in (by, cx):
            for m in ms:
                relays[m].pass_on()
        for relays, at, places in ((by, at_b, yj), (cx, at_c, xj)):
            for m in ms:
                relays[m].wait_near()
                put(at(places(1), zj(m)))
                put(at(places(3), zj(m)))

    def spread(*ms):
        for m in ms:
            b_z[m].wait_recv()
            at = pm.at[zj(m), yh, :, cols(4096 * c + col_b, 256)]
            b_last[m] = [send(at, at, device(xj(k), y, z, c)) for k in (2, 1, 3)]
            c_z[m].wait_recv()
            at = pm.at[zj(m), yh, :, cols(4096 * c + col_c, 256)]
            c_last[m] = [send(at, at, device(x, yj(k), z, c)) for k in (2, 1, 3)]

    def whole(*ms):
        for m in ms:
            for copy in b_last[m]:
                copy.wait_recv()
            by[m].start()
            for copy in c_last[m]:
                copy.wait_recv()
            cx[m].start()

    spread(1, 7)
    own_b.wait()
    own_c.wait()
    whole(0)
    spread(2, 6)
    for copy in ya_copies:
        copy.wait_recv()
    gather_a.start()
    put_a(z)
    drain(past)
    past = seen()
    spread(3, 5, 4)
    whole(1, 7)
    whole(2, 6)
    relays_pass(0)
    gather_a.pass_on(1)
    put_a(zj(7))
    put_a(zj(1))
    at_ta, at_tb, at_tc = (totals.at[:, cols(o, w)] for o, w in ((col_a, 640), (1280 + col_b, 256), (1280 + col_c, 256)))
    total_copies = [send(at_ta, at_ta, device(x, y_twin, z, c))]
    for k in range(4):
        for yy in (y, y_twin):
            if k or yy is not y:
                total_copies.append(send(at_tb, at_tb, device(xj(k), yy, z, c)))
                total_copies.append(send(at_tc, at_tc, device(xj(k), yy, z, c)))
    relays_pass(1, 7)
    drain(past)
    past = seen()
    whole(3, 5, 4)
    put_b(y)
    put(at_c(x, slice(None)))
    gather_a.pass_on(2)
    put_a(zj(6))
    put_a(zj(2))
    relays_pass(2, 6)
    relays_pass(3, 5)
    gather_a.pass_on(3)
    put_a(zj(5))
    put_a(zj(3))
    relays_pass(4)

    drain(past)
    past = seen()
    for copy in total_copies:
        copy.wait_recv()
    row_copies = []
    for first, width, out in ((0, 640, total_v), (640, 640, total_a), (1280, 4096, total_m)):
        at = out.at[:, cols(width * c, width)]
        row_copies.append(load(totals.at[mine, pl.ds(first, width)], at))
        row_copies.append(send(totals.at[theirs, pl.ds(first, width)], at, core))
    for m in (0, 1, 7, 2, 6):
        by[m].far.wait_recv()
        put(at_b(yj(2), zj(m)))
        cx[m].far.wait_recv()
        put(at_c(xj(2), zj(m)))
    for copy in row_copies:
        if copy.is_remote:
            copy.wait_recv()
        else:
            copy.wait()

    def update_state(total, state, t, at):
        new = adamw_update(total[:, at], state[0, :, at], state[1, :, at], state[2, :, at], t, 256.0)
        for k in range(3):
            state[k, :, at] = new[k]

    update_state(total_v, state_v, t_vision, pl.ds(0, 1280))
    update_state(total_a, state_a, t_audio, pl.ds(0, 1280))

    def update_columns(i, _):
        update_state(total_m, state_m, t_lm, cols(i * 1024, 1024))
        return 0

    lax.fori_loop(0, 8, update_columns, 0)
    new_states = ((mv_out, ma_out, ml_out), (nv_out, na_out, nl_out), (sv_out, sa_out, sl_out))
    for k, (v, a, m) in enumerate(new_states):
        outs += [load(state_v.at[k], v), load(state_a.at[k], a), load(state_m.at[k], m)]
    drain(past)
    for m in (3, 5, 4):
        by[m].far.wait_recv()
        put(at_b(yj(2), zj(m)))
        cx[m].far.wait_recv()
        put(at_c(xj(2), zj(m)))
    gather_a.wait()
    put_a(zj(4))
    for copy in outs:
        if copy.is_remote:
            copy.wait_recv()
        else:
            copy.wait()
    drain(seen())


def whole_step(grads, states, step_counts):
    bf, f32 = jnp.bfloat16, jnp.float32
    vm = pltpu.VMEM
    scratch = [
        vm((8, 2, 16, 640), bf), vm((8, 2, 16, 640), bf), vm((8, 2, 16, 4096), bf),
        vm((8, 2, 16, 640), bf), vm((8, 2, 16, 640), bf), vm((4, 8, 16, 1024), bf), vm((4, 8, 2, 16, 512), bf),
        vm((8, 2, 16, 1280), f32), vm((4, 8, 2, 16, 512), f32), vm((4, 8, 2, 16, 512), f32),
        vm((4, 2, 16, 1280), f32), vm((4, 2, 16, 1280), f32),
        *[vm((8, 16, 512), f32), vm((8, 16, 512), f32), vm((8, 2, 16, 512), f32), vm((8, 2, 16, 512), f32)] * 2,
        vm((2, 16, 1280), f32), vm((3, 16, 640), f32), vm((4, 16, 640), f32),
        *[vm((4, 2, 16, 512), f32)] * 4,
        *[vm((2, 16, 512), f32), vm((3, 16, 256), f32)] * 2,
        vm((3, 2, 16, 640), f32), vm((3, 16, 256), f32), vm((3, 16, 256), f32),
        vm((3, 8, 1280), f32), vm((3, 8, 1280), f32), vm((3, 8, 8192), f32),
        vm((16, 5376), f32), vm((8, 1280), f32), vm((8, 1280), f32), vm((8, 8192), f32),
        vm((8, 2, 16, 1280), bf), vm((16, 256), bf), vm((16, 256), bf),
        pltpu.SMEM((3,), jnp.int32),
        pltpu.SemaphoreType.DMA((N_SEMS,)),
    ]
    anywhere, hbm = pl.BlockSpec(memory_space=pl.ANY), pl.BlockSpec(memory_space=pltpu.HBM)
    shapes = [((8, 2, 16, g.shape[-1]), bf) for g in grads] + [(s.shape, f32) for s in states]
    return pl.pallas_call(
        step_kernel,
        out_shape=[pltpu.VMEM(*s) for s in shapes],
        in_specs=[hbm] * 13,
        out_specs=[anywhere] * 12,
        scratch_shapes=scratch,
        compiler_params=pltpu.CompilerParams(
            collective_id=0, has_side_effects=True, vmem_limit_bytes=32 * 2**20
        ),
        name="sum_update_gather",
    )(*[pltpu.with_memory_space_constraint(a, pltpu.HBM) for a in (*grads, *states, step_counts)])


def copy_kernel(*refs):
    n = len(refs) // 2
    sems = refs[-1]
    pairs = list(zip(refs[:n], refs[n:-1]))
    src, dst = pairs.pop(2)
    pairs = [(src.at[pl.ds(k, 2)], dst.at[pl.ds(k, 2)]) for k in (0, 2, 4, 6)] + pairs
    copies = [pltpu.make_async_copy(src, dst, sems.at[k]) for k, (src, dst) in enumerate(pairs)]
    for copy in copies:
        copy.start()
    for copy in copies:
        copy.wait()


def copy_out(arrays):
    n = len(arrays)
    anywhere = pl.BlockSpec(memory_space=pl.ANY)
    return pl.pallas_call(
        copy_kernel,
        out_shape=[pltpu.HBM(a.shape, a.dtype) for a in arrays],
        in_specs=[anywhere] * n,
        out_specs=[anywhere] * n,
        scratch_shapes=[pltpu.SemaphoreType.DMA((n + 3,))],
        compiler_params=pltpu.CompilerParams(vmem_limit_bytes=2**20),
        name="copy_out",
    )(*[pltpu.with_memory_space_constraint(a, pltpu.VMEM) for a in arrays])


def per_device(*arguments):
    grads, states, step_counts = arguments[:3], arguments[3:12], arguments[12]
    grads = [g.reshape(8, 2, 16, g.shape[-1]) for g in grads]
    results = copy_out(whole_step(grads, states, step_counts))
    return (*[p.reshape(256, p.shape[-1]) for p in results[:3]], *results[3:])


def solution(mesh):
    grad, state = P("replica", "shard", None, None), P("shard", None)
    return jax.shard_map(
        per_device,
        mesh=mesh,
        in_specs=(grad,) * 3 + (state,) * 9 + (P(),),
        out_specs=(P(),) * 3 + (state,) * 9,
        check_vma=False,
    )
```
